32 devices in a mesh: seq: 8 (over z, x), head: 4 (over y, core).
Axes of the slice: x: 2, y: 2, z: 4, core: 2. Of those that a mesh axis runs over, the one named last changes fastest.
Arguments:
- tokens: bfloat16 [8192, 1024], P(('seq', 'head')), may hold values from -6 to 6
- norm_gain: float32 [1024], replicated, may hold values from 0.5 to 1.5
- w_qkv: bfloat16 [1024, 8, 384], P(None, 'head'), may hold values from -0.1875 to 0.1875
- w_mem_gates: bfloat16 [8, 3, 128], P('head'), may hold values from -0.5 to 0.5
- persist_keys: bfloat16 [16, 1024], P(None, 'head'), may hold values from -6 to 6
- persist_values: bfloat16 [16, 1024], P(None, 'head'), may hold values from -6 to 6
- alpha_bias: float32 [8], P('head'), may hold values from -8 to -2
- eta_bias: float32 [8], P('head'), may hold values from -1 to 3
- w_out: bfloat16 [1024, 1024], P('head'), may hold values from -0.1875 to 0.1875
- ffn_gain: float32 [1024], replicated, may hold values from 0.5 to 1.5
- w_gate: bfloat16 [1024, 2816], replicated, may hold values from -0.1875 to 0.1875
- w_up: bfloat16 [1024, 2816], replicated, may hold values from -0.1875 to 0.1875
- w_down: bfloat16 [2816, 1024], replicated, may hold values from -0.109375 to 0.109375
- segment_ids: int32 [8192], replicated, may hold values from 0 to 3, as said below
- block_table: int32 [128], replicated, may hold values from 0 to 127, as said below
Outputs:
- mixed: bfloat16 [8192, 1024], P(('seq', 'head'))
- kv_cache: bfloat16 [128, 64, 2048], P('seq', None, 'head')
The draws below stay inside these ranges and needn't reach their ends.
Inputs may be any that keep to these rules, and one draw needn't show every extreme that they name: `segment_ids`: segment numbers never fall along the stream and change only at multiples of 64 tokens; all 4 numbers occur, and one prompt holds exactly 4096 tokens. `block_table`: A permutation of the cache rows. Row r belongs to owner r // 16; the 16 blocks of each index of seq (blocks i * 16 to (i + 1) * 16 - 1) put exactly 2 blocks with every owner.
All inputs are finite; a program needn't handle non-finite values.
Results may differ from the reference program's by a relative error of at most 0.02.
Values may be sent and summed in bfloat16 or wider, within the bound.
No kernel may reach another device: no remote copies, remote signals or barrier semaphores. Data moves between devices by JAX's collectives and lax.ppermute only.
A program may use at most 128 MiB of HBM per device.

```python
import jax
import jax.numpy as jnp
from jax import lax

D = 1024
H = 8
HD = 128
FF = 2816
PERS = 16
SPAN = 64
SEGS = 4
TOKENS = 8192
BLOCKS = 128
BPS = 16
PER_OWNER = 2
N_SEQ = 8


def draw_segment_ids(key, part):
    blocks = TOKENS // SPAN
    half = blocks // 2
    first_key, second_key = jax.random.split(jax.random.fold_in(key, 11))
    cuts = jnp.sort(jax.random.permutation(first_key, half - 1)[:SEGS - 2] + 1)
    bounds = jnp.concatenate([jnp.zeros((1,), jnp.int32), cuts.astype(jnp.int32), jnp.full((1,), half, jnp.int32)])
    others = bounds[1:] - bounds[:-1]
    spot = jax.random.randint(second_key, (), 1, SEGS - 1)
    pieces = []
    for place in range(SEGS):
        before = others[min(place, SEGS - 2)]
        after = others[max(place - 1, 0)]
        pieces.append(jnp.where(place < spot, before, jnp.where(place == spot, half, after)))
    lengths = jnp.stack(pieces).astype(jnp.int32)
    ends = jnp.cumsum(lengths)
    block_ids = jnp.arange(blocks, dtype=jnp.int32)
    numbers = jnp.sum((block_ids[:, None] >= ends[None, :SEGS - 1]).astype(jnp.int32), axis=1)
    return jnp.repeat(numbers, SPAN).astype(jnp.int32)


def draw_block_table(key, part):
    sender_keys = jax.random.split(jax.random.fold_in(key, 21), N_SEQ)
    owner_keys = jax.random.split(jax.random.fold_in(key, 22), N_SEQ)
    sender_perms = jax.vmap(lambda piece: jax.random.permutation(piece, BPS))(sender_keys)
    owner_perms = jax.vmap(lambda piece: jax.random.permutation(piece, BPS))(owner_keys)
    owners = sender_perms % N_SEQ
    copies = sender_perms // N_SEQ
    senders = jnp.arange(N_SEQ, dtype=jnp.int32)[:, None]
    local_rows = owner_perms[owners, senders * PER_OWNER + copies]
    return (owners * BPS + local_rows).reshape(-1).astype(jnp.int32)


def block_levels(key, shape, cuts, low, top_value):
    loudness, own = 1.0, jax.random.fold_in(key, 6)
    for dim, shards_of in cuts:
        heights = jnp.exp(jax.random.uniform(jax.random.fold_in(own, dim), (shards_of,), jnp.float32, low / len(cuts), top_value / len(cuts)))
        loudness = loudness * jnp.repeat(heights, shape[dim] // shards_of).reshape([-1 if axis == dim else 1 for axis in range(len(shape))])
    return loudness


def centred(key, extent, deviation, limit, cuts=(), held_as=jnp.bfloat16):
    drawn = jax.random.normal(key, extent, jnp.float32) * deviation
    if len(cuts) > 0:
        drawn = block_levels(key, extent, cuts, -0.22, 0.18) * drawn
    return jnp.clip(drawn, min=-limit, max=limit).astype(held_as)


def setup_inputs(seed: int = 0) -> dict:
    splits = jax.random.split(jax.random.key(seed), 16)
    return {
        "tokens": centred(splits[0], (TOKENS, D), 1.0, 6.0, ((0, 32),)),
        "norm_gain": jnp.clip(1.0 + 0.1 * jax.random.normal(splits[1], (D,), jnp.float32), 0.5, 1.5),
        "w_qkv": centred(splits[2], (D, H, 3 * HD), D ** -0.5, 0.1875, ((1, 4),)),
        "w_mem_gates": centred(splits[3], (H, 3, HD), HD ** -0.5, 0.5, ((0, 4),)),
        "persist_keys": centred(splits[4], (PERS, H * HD), 1.0, 6.0, ((1, 4),)),
        "persist_values": centred(splits[5], (PERS, H * HD), 1.0, 6.0, ((1, 4),)),
        "alpha_bias": jnp.clip(-8.0 + 6.0 * jax.random.uniform(splits[6], (H,), jnp.float32) ** block_levels(splits[6], (H,), ((0, 4),), -0.2, 0.2), -8.0, -2.0),
        "eta_bias": jnp.clip(-1.0 + 4.0 * jax.random.uniform(splits[7], (H,), jnp.float32) ** block_levels(splits[7], (H,), ((0, 4),), -0.2, 0.2), -1.0, 3.0),
        "w_out": centred(splits[8], (H * HD, D), (H * HD) ** -0.5, 0.1875, ((0, 4),)),
        "ffn_gain": jnp.clip(1.0 + 0.1 * jax.random.normal(splits[9], (D,), jnp.float32), 0.5, 1.5),
        "w_gate": centred(splits[10], (D, FF), D ** -0.5, 0.1875),
        "w_up": centred(splits[11], (D, FF), D ** -0.5, 0.1875),
        "w_down": centred(splits[12], (FF, D), FF ** -0.5, 0.109375),
        "segment_ids": draw_segment_ids(jax.random.fold_in(splits[15], 71), 0),
        "block_table": draw_block_table(jax.random.fold_in(splits[15], 71), 0),
    }


EPS = 1e-05
TINY = 1e-06
HIGH = lax.Precision.HIGHEST

def rms_scale(values, gain):
    return values * lax.rsqrt(lax.optimization_barrier(jnp.mean(values * values, axis=-1, keepdims=True)) + EPS) * gain

def rms_plain(values):
    return values * lax.rsqrt(lax.optimization_barrier(jnp.mean(values * values, axis=-1, keepdims=True)) + TINY)

def reference(tokens, norm_gain, w_qkv, w_mem_gates, persist_keys, persist_values, alpha_bias, eta_bias, w_out, ffn_gain, w_gate, w_up, w_down, segment_ids, block_table):
    resid = tokens.astype(jnp.float32)
    normed = rms_scale(resid, norm_gain).astype(jnp.bfloat16)
    projected = jnp.dot(normed, w_qkv.reshape(D, H * 3 * HD), preferred_element_type=jnp.float32)
    projected = projected.reshape(TOKENS, H, 3, HD)
    queries = rms_plain(projected[:, :, 0]) * HD ** (-0.5)
    keys = rms_plain(projected[:, :, 1]) * HD ** (-0.5)
    values = projected[:, :, 2]
    logits = jnp.einsum('thd,hgd->thg', values, w_mem_gates.astype(jnp.float32), precision=HIGH)
    theta = jax.nn.sigmoid(logits[..., 0]) / SPAN
    alpha = jax.nn.sigmoid(lax.optimization_barrier(jnp.mean(logits[..., 1].reshape(BLOCKS, SPAN, H), axis=1)) + alpha_bias)
    eta = jax.nn.sigmoid(lax.optimization_barrier(jnp.mean(logits[..., 2].reshape(BLOCKS, SPAN, H), axis=1)) + eta_bias)
    id_blocks = segment_ids.reshape(BLOCKS, SPAN)
    keep = jnp.concatenate([jnp.zeros((1,), jnp.float32), (id_blocks[1:, 0] == id_blocks[:-1, -1]).astype(jnp.float32)])
    pkeys = persist_keys.astype(jnp.float32).reshape(PERS, H, HD)
    pvals = persist_values.astype(jnp.float32).reshape(PERS, H, HD)
    initial = jnp.einsum('phd,phe->hde', pkeys, pvals, precision=HIGH) / PERS

    def span_step(carry, item):
        memory, moment = carry
        qry, key_rows, val_rows, weight, forget, carry_rate, kept = item
        held = kept * memory + (1.0 - kept) * initial
        moment_in = kept * moment
        recalled = jnp.einsum('thd,hde->the', qry, held, precision=HIGH)
        gram = jnp.einsum('th,thd,the->hde', weight, key_rows, key_rows, precision=HIGH)
        cross = jnp.einsum('th,thd,the->hde', weight, key_rows, val_rows, precision=HIGH)
        moment = carry_rate[:, None, None] * moment_in - jnp.einsum('hde,hef->hdf', gram, held, precision=HIGH) + cross
        memory = (1.0 - forget)[:, None, None] * held + moment
        return ((memory, moment), recalled)
    items = (queries.reshape(BLOCKS, SPAN, H, HD), keys.reshape(BLOCKS, SPAN, H, HD), values.reshape(BLOCKS, SPAN, H, HD), theta.reshape(BLOCKS, SPAN, H), alpha, eta, keep)
    start = jnp.zeros((H, HD, HD), jnp.float32)
    unused, recalled = lax.scan(span_step, (start, start), items)
    retrieved = rms_plain(recalled.reshape(TOKENS, H, HD)).astype(jnp.bfloat16).reshape(TOKENS, H * HD)
    residual = resid + jnp.dot(retrieved, w_out, preferred_element_type=jnp.float32)
    ffn_in = rms_scale(residual, ffn_gain).astype(jnp.bfloat16)
    gate = jnp.dot(ffn_in, w_gate, preferred_element_type=jnp.float32)
    upper = jnp.dot(ffn_in, w_up, preferred_element_type=jnp.float32)
    hidden = (jax.nn.silu(gate) * upper).astype(jnp.bfloat16)
    mixed = (residual + jnp.dot(hidden, w_down, preferred_element_type=jnp.float32)).astype(jnp.bfloat16)
    pairs = jnp.stack([keys, values], axis=2).astype(jnp.bfloat16).reshape(BLOCKS, SPAN, 2 * H * HD)
    kv_cache = jnp.zeros((BLOCKS, SPAN, 2 * H * HD), jnp.bfloat16).at[block_table].set(pairs)
    return (mixed, kv_cache)
```

```python
import functools

import jax
import jax.numpy as jnp
from jax import lax
from jax.experimental import pallas as pl
from jax.experimental.pallas import tpu as pltpu
from jax.sharding import PartitionSpec as P

PERS = 16
SPAN = 64
EPS = 1e-05
TINY = 1e-06
BF = jnp.bfloat16
F32 = jnp.float32
SCALE = 0.001
VMEM_LIMIT = 12 * 1024 * 1024
MOST_VMEM = 60 * 1024 * 1024
CUTS = 2


def dot(a, b):
    return jnp.dot(a, b, preferred_element_type=F32)


def vmem():
    return pl.BlockSpec(memory_space=pltpu.VMEM)


def smem():
    return pl.BlockSpec(memory_space=pltpu.SMEM)


def loaded(shape):
    return pl.BlockSpec(shape, lambda i: (0,) * len(shape))


def exchange(value, axis, bit):
    count = lax.axis_size(axis)
    return lax.ppermute(value, axis, [(i, i ^ bit) for i in range(count)])


def params(limit=VMEM_LIMIT):
    return pltpu.CompilerParams(vmem_limit_bytes=limit)


def cost(flops, size):
    return pl.CostEstimate(flops=int(flops * SCALE), bytes_accessed=int(size * SCALE), transcendentals=0)


def compose(later, earlier):
    d = later.shape[0] // 2
    joined = dot(later[:, : 2 * d].astype(BF), earlier.astype(BF))
    shift = joined[:, 2 * d :] + later[:, 2 * d :].astype(F32)
    return jnp.concatenate([joined[:, : 2 * d], shift], axis=1)


def ordered(flag, one, other):
    swap = flag != 0
    return jnp.where(swap, other, one), jnp.where(swap, one, other)


def rms_plain(values):
    return values * lax.rsqrt(jnp.mean(values * values, axis=-1, keepdims=True) + TINY)


def pair_kernel(heads, d, blocks, rel, is_last, groups, parts, *refs):
    refs = list(refs)
    meta_ref, flat_ref = refs[:2]
    x_refs = [refs[2 : 2 + parts[0]], refs[2 + parts[0] : 2 + sum(parts)]]
    refs = refs[2 + sum(parts) :]
    gain_ref, w_ref, gates_ref, start_ref = refs[:4]
    others = refs[4 : 4 + groups - 1] if is_last else []
    outs = refs[4 + len(others) :]
    kv_out, r_ref, group_ref = outs[:3]
    total_refs = outs[3:-2]
    kv_ref, sem = outs[-2:]
    bias = flat_ref.shape[0] - 2 * heads
    me = meta_ref[0]
    gain = gain_ref[...]
    w = w_ref[...]
    kept = {}
    for s in range(2):
        x = jnp.concatenate([ref[...] for ref in x_refs[s]], axis=0).astype(F32)
        scale = lax.rsqrt(jnp.mean(x * x, axis=-1, keepdims=True) + EPS)
        projected = dot((x * scale * gain).astype(BF), w)
        base = (me ^ (rel + s)) * blocks
        for h in range(heads):
            q = projected[:, 3 * d * h : 3 * d * h + d]
            k = projected[:, 3 * d * h + d : 3 * d * h + 2 * d]
            v = projected[:, 3 * d * h + 2 * d : 3 * d * h + 3 * d]
            q = rms_plain(q) * d**-0.5
            k = rms_plain(k) * d**-0.5
            kb, vb = k.astype(BF), v.astype(BF)
            logits = dot(vb, gates_ref[h])
            theta = jax.nn.sigmoid(logits[:, :d]) * (1.0 / SPAN)
            weighted = (theta * k).astype(BF)
            both = jnp.concatenate([kb, vb], axis=1)
            items = []
            for c in range(blocks):
                part = slice(c * SPAN, (c + 1) * SPAN)
                kv_ref[s * blocks + c, :, 2 * d * h : 2 * d * (h + 1)] = both[part]
                products = lax.dot_general(
                    weighted[part], both[part], (((0,), (0,)), ((), ())), preferred_element_type=F32
                )
                alpha = jax.nn.sigmoid(jnp.mean(logits[part, d : 2 * d], axis=0, keepdims=True) + flat_ref[bias + h])
                eta = jax.nn.sigmoid(
                    jnp.mean(logits[part, 2 * d :], axis=0, keepdims=True) + flat_ref[bias + heads + h]
                )
                widen = lambda row: jnp.concatenate([row, row, row], axis=1)
                items.append((products, widen(1.0 - alpha), widen(eta), q[part].astype(BF), flat_ref[base + c]))
            kept[s, h] = items
    copies = [pltpu.make_async_copy(kv_ref, kv_out, sem.at[0])]
    copies[0].start()
    zero = jnp.zeros((d, d), F32)
    row = lax.broadcasted_iota(jnp.int32, (d, d), 0)
    column = lax.broadcasted_iota(jnp.int32, (d, d), 1)
    eye = jnp.where(row == column, 1.0, 0.0).astype(F32)
    state = {}
    starts = []
    for h in range(heads):
        first = start_ref[h]
        starts.append(jnp.concatenate([zero, zero, first], axis=1))
    for key in kept:
        state[key] = (jnp.concatenate([eye, zero, zero], axis=1), jnp.concatenate([zero, eye, zero], axis=1))
    for c in range(blocks):
        for s in range(2):
            for h in range(heads):
                products, stay, eta, q, keep = kept[s, h][c]
                memory, moment = state[s, h]
                held = keep * memory + (1.0 - keep) * starts[h]
                held_low = held.astype(BF)
                recalled = dot(q, held_low)
                part = slice(c * SPAN, (c + 1) * SPAN)
                r_ref[s, h, part, :] = recalled
                cross = jnp.concatenate([zero, zero, products[:, d:]], axis=1)
                moment = eta * (keep * moment) - dot(products[:, :d].astype(BF), held_low) + cross
                state[s, h] = (stay * held + moment, moment)
    late = 1 - (me & 1)
    for h in range(heads):
        maps = [jnp.concatenate(state[s, h], axis=0) for s in range(2)]
        earlier, later = ordered(me & 1, maps[0], maps[1])
        low = earlier.astype(BF)
        total = compose(later, low)
        group_ref[h] = total.astype(BF)
        if is_last:
            level = [others[g][h] for g in range(groups - 1)] + [total]
            bit = 2
            while len(level) > 1:
                joined = []
                for i in range(0, len(level), 2):
                    earlier, later = ordered(me & bit, level[i].astype(F32), level[i + 1].astype(F32))
                    joined.append(compose(later, earlier))
                level = joined
                bit *= 2
            for i in range(2):
                total_refs[2 * h + i][...] = level[0][i * d : (i + 1) * d].astype(BF)
        recalled = r_ref[late, h]
        folded = dot(recalled[:, : 2 * d].astype(BF), low)
        r_ref[late, h, :, : 2 * d] = folded[:, : 2 * d]
        r_ref[late, h, :, 2 * d :] = folded[:, 2 * d :] + recalled[:, 2 * d :]
    for one in copies:
        one.wait()


def pair_call(meta, flat, xs, gain, w, gates, initial, rel, before, is_last):
    heads, d = gates.shape[0], gates.shape[1]
    parts = [len(x) for x in xs]
    rows = sum(x.shape[0] for x in xs[0])
    blocks = rows // SPAN
    groups = len(before) + 1
    extra = [b["map"] for b in before] if is_last else []
    hbm = pl.BlockSpec(memory_space=pltpu.HBM)
    row = heads * 2 * d
    shapes = [
        jax.ShapeDtypeStruct((2 * blocks, SPAN, row), BF),
        jax.ShapeDtypeStruct((2, heads, rows, 3 * d), F32),
        jax.ShapeDtypeStruct((heads, 2 * d, 3 * d), BF),
    ]
    specs = [hbm, vmem(), vmem()]
    if is_last:
        shapes += [jax.ShapeDtypeStruct((d, 3 * d), BF)] * (2 * heads)
        specs += [vmem()] * (2 * heads)
    out = pl.pallas_call(
        functools.partial(pair_kernel, heads, d, blocks, rel, is_last, groups, parts),
        out_shape=shapes,
        grid=(1,),
        in_specs=[smem()] * 2
        + [vmem()] * (sum(parts) + 4)
        + [vmem()] * len(extra),
        out_specs=specs,
        scratch_shapes=[
            pltpu.VMEM((2 * blocks, SPAN, row), BF),
            pltpu.SemaphoreType.DMA((1,)),
        ],
        compiler_params=params(),
        cost_estimate=cost(2.5e9, 8e6),
        name="pair_last" if is_last else "pair_first",
    )(meta, flat, *xs[0], *xs[1], gain, w, gates, initial, *extra)
    names = ["kv", "r", "map"]
    return dict(zip(names, out), total=out[3:])


def join_kernel(heads, d, seq_ref, *refs):
    own_refs, got_refs, (a_ref, b_ref, got_ref) = refs[: 2 * heads], refs[2 * heads : 4 * heads], refs[4 * heads :]
    for h in range(heads):
        own, got = (
            jnp.concatenate([ref[...] for ref in side[2 * h : 2 * h + 2]], axis=0) for side in (own_refs, got_refs)
        )
        earlier, later = ordered(seq_ref[0] & 1, own.astype(F32), got.astype(F32))
        joined = compose(later, earlier).astype(BF)
        a_ref[h] = joined[:, : 2 * d]
        b_ref[h] = joined[:, 2 * d :]
        got_ref[h] = got


def join(seq, own, got):
    heads, d = len(own) // 2, own[0].shape[0]
    shapes = [(heads, 2 * d, 2 * d), (heads, 2 * d, d), (heads, 2 * d, 3 * d)]
    return pl.pallas_call(
        functools.partial(join_kernel, heads, d),
        out_shape=[jax.ShapeDtypeStruct(shape, BF) for shape in shapes],
        in_specs=[smem()] + [vmem()] * (4 * heads),
        out_specs=[vmem()] * 3,
        compiler_params=params(),
        cost_estimate=cost(1e8, 1.2e6),
        name="join",
    )(seq, *own, *got)


def step_kernel(heads, a_ref, b_ref, state_ref, out_ref):
    for h in range(heads):
        out_ref[h] = (dot(a_ref[h], state_ref[h]) + b_ref[h].astype(F32)).astype(BF)


def step(a, b, state):
    return pl.pallas_call(
        functools.partial(step_kernel, a.shape[0]),
        out_shape=jax.ShapeDtypeStruct(b.shape, BF),
        in_specs=[vmem()] * 3,
        out_specs=vmem(),
        compiler_params=params(),
        cost_estimate=cost(1e8, 6e5),
        name="step",
    )(a, b, state)


def fold_kernel(heads, d, groups, *refs):
    meta_ref, seq_ref, got_ref = refs[:3]
    map_refs, r_refs = (refs[3 + i * groups : 3 + (i + 1) * groups] for i in range(2))
    out_ref, out0_ref = refs[3 + 2 * groups :]
    me, odd = meta_ref[0], (seq_ref[0] & 1) != 0
    d2 = 2 * d
    shape = (d2, 3 * d)
    identity = jnp.where(
        lax.broadcasted_iota(jnp.int32, shape, 0) == lax.broadcasted_iota(jnp.int32, shape, 1), 1.0, 0.0
    ).astype(F32)
    fronts = []
    for h in range(heads):
        before = [jnp.where(odd, got_ref[h].astype(F32), identity)] * groups
        own = [identity] * groups
        level = [map_refs[g][h].astype(F32) for g in range(groups)]
        bit, span = 2, 1
        while len(level) > 1:
            joined = []
            for i in range(0, len(level), 2):
                for side in range(2):
                    active = (me & bit) != side * bit
                    sibling = level[i + 1 - side]
                    for g in range((i + side) * span, (i + side + 1) * span):
                        after = sibling if span == 1 else compose(own[g], sibling)
                        own[g] = jnp.where(active, after, own[g])
                if len(level) > 2:
                    earlier, later = ordered(me & bit, level[i], level[i + 1])
                    joined.append(compose(later, earlier))
                else:
                    joined.append(None)
            level = joined
            bit, span = bit * 2, span * 2
        fronts.append([compose(own[g], before[g]).astype(BF) for g in range(groups)])
    for g in range(groups):
        for s in range(2):
            r = 2 * g + s
            for h in range(heads):
                folded = dot(r_refs[g][s, h, :, :d2].astype(BF), fronts[h][g])
                out_ref[r, h] = folded[:, :d2].astype(BF)
                out0_ref[r, h] = folded[:, d2:] + r_refs[g][s, h, :, d2:]


def fold(meta, seq, got, pairs):
    groups = len(pairs)
    _, heads, rows, width = pairs[0]["r"].shape
    d = width // 3
    shapes = [(2 * groups, heads, rows, 2 * d), (2 * groups, heads, rows, d)]
    return pl.pallas_call(
        functools.partial(fold_kernel, heads, d, groups),
        out_shape=[jax.ShapeDtypeStruct(shapes[0], BF), jax.ShapeDtypeStruct(shapes[1], F32)],
        in_specs=[smem(), smem(), vmem()] + [vmem()] * (2 * groups),
        out_specs=[vmem()] * 2,
        compiler_params=params(),
        cost_estimate=cost(1.2e9, 6e6),
        name="fold",
    )(meta, seq, got, *[p["map"] for p in pairs], *[p["r"] for p in pairs])


def recall_kernel(heads, d, shards, r_ref, r0_ref, state_ref, *out_refs):
    for r in reversed(range(shards)):
        for h in range(heads):
            recalled = dot(r_ref[r, h], state_ref[h]) + r0_ref[r, h]
            out_refs[r][:, h * d : (h + 1) * d] = rms_plain(recalled).astype(BF)


def recall(r, r0, state):
    shards, heads, rows, width = r.shape
    d = width // 2
    return pl.pallas_call(
        functools.partial(recall_kernel, heads, d, shards),
        out_shape=[jax.ShapeDtypeStruct((rows, heads * d), BF)] * shards,
        in_specs=[vmem()] * 3,
        out_specs=[vmem()] * shards,
        compiler_params=params(),
        cost_estimate=cost(2e8, 3e6),
        name="recall",
    )(r, r0, state)


def ffn_kernel(shards, tile, *refs):
    sources, out_ref, targets = refs[: 2 * shards + 5], refs[2 * shards + 5], refs[2 * shards + 6 : -3]
    hidden_ref, residual_ref, sem = refs[-3:]
    wg_ref, wu_ref, wd_ref = targets[-3:]
    small = [
        pltpu.make_async_copy(source, target, sem.at[i])
        for i, (source, target) in enumerate(zip(sources[:-3], targets[:-3]))
    ]
    down = pltpu.make_async_copy(sources[-1], wd_ref, sem.at[len(small)])
    columns = []
    for i in range(wg_ref.shape[1] // tile):
        part = pl.ds(i * tile, tile)
        at = len(small) + 1 + 2 * i
        columns.append(
            [
                pltpu.make_async_copy(sources[-3].at[:, part], wg_ref.at[:, part], sem.at[at]),
                pltpu.make_async_copy(sources[-2].at[:, part], wu_ref.at[:, part], sem.at[at + 1]),
            ]
        )
    for one in small + [one for pair in columns for one in pair] + [down]:
        one.start()
    for one in small:
        one.wait()
    x_ref, gain_ref = targets[:2]
    residual = x_ref[...].astype(F32)
    for r in range(shards):
        residual += dot(targets[2 + r][...], targets[2 + shards + r][...])
    residual_ref[...] = residual
    scale = lax.rsqrt(jnp.mean(residual * residual, axis=-1, keepdims=True) + EPS)
    low = (residual * scale * gain_ref[...]).astype(BF)
    for i, pair in enumerate(columns):
        for one in pair:
            one.wait()
        part = slice(i * tile, (i + 1) * tile)
        gate = dot(low, wg_ref[:, part])
        up = dot(low, wu_ref[:, part])
        hidden_ref[:, part] = (gate / (1.0 + jnp.exp(-gate)) * up).astype(BF)
    down.wait()
    out_ref[...] = (residual_ref[...] + dot(hidden_ref[...], wd_ref[...])).astype(BF)


def ffn(x, gain, w_out, pieces, w_gate, w_up, w_down):
    rows, width = x.shape
    hidden = w_gate.shape[1]
    tile = 256
    while hidden % tile:
        tile //= 2
    shards = len(pieces)
    sources = [x, gain, *pieces, *w_out, w_gate, w_up, w_down]
    return pl.pallas_call(
        functools.partial(ffn_kernel, shards, tile),
        out_shape=jax.ShapeDtypeStruct((rows, width), BF),
        in_specs=[pl.BlockSpec(memory_space=pl.ANY)] * len(sources),
        out_specs=vmem(),
        scratch_shapes=[pltpu.VMEM(a.shape, a.dtype) for a in sources]
        + [
            pltpu.VMEM((rows, hidden), BF),
            pltpu.VMEM((rows, width), F32),
            pltpu.SemaphoreType.DMA((2 * shards + 3 + 2 * (hidden // tile),)),
        ],
        compiler_params=params(MOST_VMEM),
        cost_estimate=cost(5e9, 2.2e7),
        name="ffn",
    )(*sources)


def pack_kernel(groups, order_ref, *refs):
    kv_refs, targets, (stage, sem_in, sem_out) = refs[:groups], refs[groups:-3], refs[-3:]
    count = kv_refs[0].shape[0]
    into = [
        pltpu.make_async_copy(kv_refs[g], stage.at[pl.ds(g * count, count)], sem_in.at[g]) for g in range(groups)
    ]
    out = []
    for target in targets:
        for i in range(target.shape[0]):
            n = len(out)
            out.append(pltpu.make_async_copy(stage.at[order_ref[n]], target.at[i], sem_out.at[n]))
    for one in into:
        one.start()
    for one in into:
        one.wait()
    for one in out:
        one.start()
    for one in out:
        one.wait()


def pack(order, kv, counts):
    hbm = pl.BlockSpec(memory_space=pltpu.HBM)
    blocks = sum(counts)
    block = kv[0].shape[1:]
    return pl.pallas_call(
        functools.partial(pack_kernel, len(kv)),
        out_shape=[jax.ShapeDtypeStruct((n,) + block, BF) for n in counts],
        in_specs=[smem()] + [hbm] * len(kv),
        out_specs=[hbm] * len(counts),
        scratch_shapes=[
            pltpu.VMEM((blocks,) + block, BF),
            pltpu.SemaphoreType.DMA((len(kv),)),
            pltpu.SemaphoreType.DMA((blocks,)),
        ],
        compiler_params=params(),
        cost_estimate=cost(0, 4e6),
        name="pack",
    )(order, *kv)


def place_kernel(rows_ref, *refs):
    sources, (out_ref, stage, sem_in, sem_out) = refs[:-4], refs[-4:]
    into, out = [], []
    for source in sources:
        for i in range(source.shape[0]):
            n = len(into)
            into.append(pltpu.make_async_copy(source.at[i], stage.at[n], sem_in.at[n]))
            out.append(pltpu.make_async_copy(stage.at[n], out_ref.at[rows_ref[n]], sem_out.at[n]))
    for one in into:
        one.start()
    for first, second in zip(into, out):
        first.wait()
        second.start()
    for one in out:
        one.wait()


def place(rows, sources):
    anywhere = pl.BlockSpec(memory_space=pl.ANY)
    count = rows.shape[0]
    shape = (count,) + sources[0].shape[1:]
    return pl.pallas_call(
        place_kernel,
        out_shape=jax.ShapeDtypeStruct(shape, sources[0].dtype),
        in_specs=[smem()] + [anywhere] * len(sources),
        out_specs=anywhere,
        scratch_shapes=[
            pltpu.VMEM(shape, sources[0].dtype),
            pltpu.SemaphoreType.DMA((count,)),
            pltpu.SemaphoreType.DMA((count,)),
        ],
        compiler_params=params(MOST_VMEM),
        cost_estimate=cost(0, 4 * sources[0].size * len(sources)),
        name="place",
    )(rows, *sources)


def per_device(
    tokens,
    norm_gain,
    w_qkv,
    w_mem_gates,
    persist_keys,
    persist_values,
    alpha_bias,
    eta_bias,
    w_out,
    ffn_gain,
    w_gate,
    w_up,
    w_down,
    segment_ids,
    block_table,
):
    model_dim = tokens.shape[1]
    heads, d = w_qkv.shape[1], w_mem_gates.shape[2]
    shards = lax.axis_size("head")
    n_seq = lax.axis_size("seq")
    seq_index, head_index = lax.axis_index("seq"), lax.axis_index("head")
    blocks_here = shards * tokens.shape[0] // SPAN
    per_owner = blocks_here // n_seq

    count = tokens.shape[0] // SPAN
    cut = tokens.shape[0] // CUTS
    parts = [tokens[i * cut : (i + 1) * cut] for i in range(CUTS)]
    far = [[exchange(part, "head", 2 * g) for part in parts] for g in range(1, shards // 2)]
    xs = {0: [parts, [exchange(tokens, "head", 1)]]}

    int32 = jnp.int32
    half = blocks_here // 2
    parity, place_in_line = seq_index & 1, seq_index >> 1
    id_blocks = segment_ids.reshape(-1, SPAN)[:, 0]
    keep_all = jnp.concatenate([jnp.zeros((1,), F32), (id_blocks[1:] == id_blocks[:-1]).astype(F32)])
    keep = lax.dynamic_slice_in_dim(keep_all, seq_index * blocks_here, blocks_here)
    flat = jnp.concatenate([keep, alpha_bias, eta_bias])
    meta = head_index.astype(int32)[None]
    seq = seq_index.astype(int32)[None]

    gates = jnp.broadcast_to(
        jnp.transpose(w_mem_gates, (0, 2, 1))[:, :, :, None], (heads, d, 3, d)
    ).reshape(heads, d, 3 * d)
    w = w_qkv.reshape(model_dim, heads * 3 * d)
    gain = norm_gain.reshape(1, -1)
    pkeys = persist_keys.reshape(PERS, heads, d)
    pvalues = persist_values.reshape(PERS, heads, d)
    initial = jnp.einsum("phd,phe->hde", pkeys, pvalues, preferred_element_type=F32) / PERS

    pairs = []
    groups = shards // 2
    for g in range(groups):
        if g > 0:
            far[g - 1], pairs[0]["map"] = lax.optimization_barrier((far[g - 1], pairs[0]["map"]))
            xs[g] = [far[g - 1], [exchange(part, "head", 1) for part in far[g - 1]]]
        pairs.append(pair_call(meta, flat, xs[g], gain, w, gates, initial, 2 * g, pairs, g == groups - 1))
    total, block_table, w_out = lax.optimization_barrier((pairs[-1]["total"], block_table, w_out))
    w_outs = [w_out] + [exchange(w_out, "head", 2 * g) for g in range(1, groups)]
    got = [exchange(part, "seq", 1) for part in total]

    mine = lax.dynamic_slice_in_dim(block_table, seq_index * blocks_here, blocks_here)
    owners = mine // blocks_here
    slots = jnp.arange(blocks_here, dtype=int32)
    same_owner = (owners[:, None] == owners[None, :]) & (slots[None, :] < slots[:, None])
    rank = jnp.sum(same_owner.astype(int32), axis=1)
    position = ((owners & 1) ^ parity ^ 1) * half + ((owners >> 1) ^ place_in_line) * per_owner + rank
    relative = ((slots // count) ^ head_index) * count + slots % count
    order = jnp.sum(jnp.where(position[None, :] == slots[:, None], relative[None, :], 0), axis=1).astype(int32)
    to_me = (block_table // blocks_here == seq_index).reshape(n_seq, blocks_here)
    earlier = to_me[:, None, :] & (slots[None, None, :] < slots[None, :, None])
    sources = jnp.arange(n_seq, dtype=int32)[:, None]
    arrival = (
        jnp.sum(earlier.astype(int32), axis=2)
        + ((sources & 1) ^ parity ^ 1) * half
        + ((sources >> 1) ^ place_in_line) * per_owner
    )
    landed = (arrival.reshape(1, -1) == slots[:, None]) & to_me.reshape(1, -1)
    rows = jnp.sum(jnp.where(landed, (block_table % blocks_here)[None, :], 0), axis=1).astype(int32)

    line = n_seq // 2
    packed = pack(order, [p["kv"] for p in pairs], (half,) + (per_owner,) * line)
    cross, same = packed[0], list(packed[1:])
    got, cross, same = lax.optimization_barrier((got, cross, same))
    a, b, got = join(seq, total, got)
    b, cross = lax.optimization_barrier((b, cross))
    cross = exchange(cross, "seq", 1)
    r, r0 = fold(meta, seq, got, pairs)
    onward = [(i, i + 2) for i in range(n_seq - 2)]
    hops = n_seq // 4
    state = b
    for hop in range(hops):
        state = lax.ppermute(state, "seq", onward)
        if hop == 0:
            state, r, w_outs = lax.optimization_barrier((state, r, w_outs))
        if hop < hops - 1:
            state = step(a, b, state)
    state, cross = lax.optimization_barrier((state, cross))
    w_outs = [w for one in w_outs for w in (one, exchange(one, "head", 1))]
    retrieved = list(recall(r, r0, state))
    pieces = [retrieved[0]] + [exchange(retrieved[i], "head", i) for i in range(1, shards)]
    cross = [cross[m * per_owner : (m + 1) * per_owner] for m in range(line)]
    cross = cross[:1] + [exchange(cross[m], "seq", 2 * m) for m in range(1, line)]
    same = [same[m] if m == 0 else exchange(same[m], "seq", 2 * m) for m in range(line)]
    mixed = ffn(tokens, ffn_gain.reshape(1, -1), w_outs, pieces, w_gate, w_up, w_down)
    mixed, cross, same = lax.optimization_barrier((mixed, cross, same))
    kv_cache = place(rows, cross + same)
    return mixed, kv_cache


def solution(mesh):
    return jax.shard_map(
        per_device,
        mesh=mesh,
        in_specs=(
            P(("seq", "head"), None),
            P(),
            P(None, "head", None),
            P("head", None, None),
            P(None, "head"),
            P(None, "head"),
            P("head"),
            P("head"),
            P("head", None),
            P(),
            P(),
            P(),
            P(),
            P(),
            P(),
        ),
        out_specs=(P(("seq", "head"), None), P("seq", None, "head")),
        check_vma=False,
    )
```

```python
import functools

import jax
import jax.numpy as jnp
from jax import lax
from jax.experimental import pallas as pl
from jax.experimental.pallas import tpu as pltpu
from jax.sharding import PartitionSpec as P

PERS = 16
PER_OWNER = 2
SPAN = 64
EPS = 1e-05
TINY = 1e-06
BF = jnp.bfloat16
F32 = jnp.float32
SCALE = 0.001
VMEM_LIMIT = 12 * 1024 * 1024
MOST_VMEM = 60 * 1024 * 1024
STORE_BYTES = 56 * 1024 * 1024
CUTS = 1


def dot(a, b):
    return jnp.dot(a, b, preferred_element_type=F32)


def vmem():
    return pl.BlockSpec(memory_space=pltpu.VMEM)


def smem():
    return pl.BlockSpec(memory_space=pltpu.SMEM)


def loaded(shape):
    return pl.BlockSpec(shape, lambda i: (0,) * len(shape))


def exchange(value, axis, bit):
    count = lax.axis_size(axis)
    return lax.ppermute(value, axis, [(i, i ^ bit) for i in range(count)])


def params(limit=VMEM_LIMIT):
    return pltpu.CompilerParams(vmem_limit_bytes=limit)


def cost(flops, size):
    return pl.CostEstimate(flops=int(flops * SCALE), bytes_accessed=int(size * SCALE), transcendentals=0)


def compose(later, earlier):
    d = later.shape[0] // 2
    joined = dot(later[:, : 2 * d].astype(BF), earlier.astype(BF))
    shift = joined[:, 2 * d :] + later[:, 2 * d :].astype(F32)
    return jnp.concatenate([joined[:, : 2 * d], shift], axis=1)


def ordered(flag, one, other):
    swap = flag != 0
    return jnp.where(swap, other, one), jnp.where(swap, one, other)


def rms_plain(values):
    return values * lax.rsqrt(jnp.mean(values * values, axis=-1, keepdims=True) + TINY)


def pair_kernel(heads, d, blocks, rel, is_last, groups, parts, packs, *refs):
    refs = list(refs)
    meta_ref, flat_ref, slot_ref = refs[:3]
    refs = refs[3:]
    x_refs = [refs[: parts[0]], refs[parts[0] : sum(parts)]]
    refs = refs[sum(parts) :]
    gain_ref, w_ref, gates_ref, start_ref = refs[:4]
    others = refs[4 : 4 + groups - 1] if is_last else []
    kv_before = refs[4 + len(others) : 4 + 2 * len(others)]
    outs = refs[4 + 2 * len(others) + (rel > 0) :]
    store_ref, group_ref = outs[:2]
    kv_outs = outs[2 : 2 + packs]
    total_refs = outs[2 + packs : -3]
    kv_ref, r_ref, sem = outs[-3:]
    bias = flat_ref.shape[0] - 2 * heads
    me = meta_ref[0]
    if rel == 0:
        table_ref, (slot_out,) = slot_ref, total_refs
        here, total_blocks = meta_ref[1], slot_out.shape[0]
        owners = [lax.div(table_ref[here * total_blocks + c], total_blocks) for c in range(total_blocks)]
        for c, owner in enumerate(owners):
            rank = sum([jnp.where(owners[e] == owner, 1, 0) for e in range(c)], jnp.int32(0))
            place = lax.shift_right_logical(owner, 1) ^ lax.shift_right_logical(here, 1)
            cross = (owner & 1) ^ (here & 1)
            slot_out[c] = (1 - cross) * (total_blocks // 2) + place * PER_OWNER + rank
    if is_last:
        for g, source in enumerate(kv_before):
            for i in range(2 * blocks):
                kv_ref[slot_ref[(me ^ (2 * g + i // blocks)) * blocks + i % blocks]] = source[i]
    gain = gain_ref[...]
    w = w_ref[...]
    kept = {}
    for s in range(2):
        x = jnp.concatenate([ref[...] for ref in x_refs[s]], axis=0).astype(F32)
        scale = lax.rsqrt(jnp.mean(x * x, axis=-1, keepdims=True) + EPS)
        projected = dot((x * scale * gain).astype(BF), w)
        base = (me ^ (rel + s)) * blocks
        for h in range(heads):
            q = projected[:, 3 * d * h : 3 * d * h + d]
            k = projected[:, 3 * d * h + d : 3 * d * h + 2 * d]
            v = projected[:, 3 * d * h + 2 * d : 3 * d * h + 3 * d]
            q = rms_plain(q) * d**-0.5
            k = rms_plain(k) * d**-0.5
            kb, vb = k.astype(BF), v.astype(BF)
            logits = dot(vb, gates_ref[h])
            theta = jax.nn.sigmoid(logits[:, :d]) * (1.0 / SPAN)
            weighted = (theta * k).astype(BF)
            both = jnp.concatenate([kb, vb], axis=1)
            items = []
            for c in range(blocks):
                part = slice(c * SPAN, (c + 1) * SPAN)
                where = slot_ref[base + c] if is_last else s * blocks + c
                kv_ref[where, :, 2 * d * h : 2 * d * (h + 1)] = both[part]
                products = lax.dot_general(
                    weighted[part], both[part], (((0,), (0,)), ((), ())), preferred_element_type=F32
                )
                alpha = jax.nn.sigmoid(jnp.mean(logits[part, d : 2 * d], axis=0, keepdims=True) + flat_ref[bias + h])
                eta = jax.nn.sigmoid(
                    jnp.mean(logits[part, 2 * d :], axis=0, keepdims=True) + flat_ref[bias + heads + h]
                )
                widen = lambda row: jnp.concatenate([row, row, row], axis=1)
                items.append((products, widen(1.0 - alpha), widen(eta), q[part].astype(BF), flat_ref[base + c]))
            kept[s, h] = items
    copies, at = [], 0
    for target in kv_outs:
        count = target.shape[0]
        copies.append(pltpu.make_async_copy(kv_ref.at[pl.ds(at, count)], target, sem.at[len(copies)]))
        at += count
    for one in copies:
        one.start()
    zero = jnp.zeros((d, d), F32)
    row = lax.broadcasted_iota(jnp.int32, (d, d), 0)
    column = lax.broadcasted_iota(jnp.int32, (d, d), 1)
    eye = jnp.where(row == column, 1.0, 0.0).astype(F32)
    state = {}
    starts = []
    for h in range(heads):
        first = start_ref[h]
        starts.append(jnp.concatenate([zero, zero, first], axis=1))
    for key in kept:
        state[key] = (jnp.concatenate([eye, zero, zero], axis=1), jnp.concatenate([zero, eye, zero], axis=1))
    for c in range(blocks):
        for s in range(2):
            for h in range(heads):
                products, stay, eta, q, keep = kept[s, h][c]
                memory, moment = state[s, h]
                held = keep * memory + (1.0 - keep) * starts[h]
                held_low = held.astype(BF)
                recalled = dot(q, held_low)
                part = slice(c * SPAN, (c + 1) * SPAN)
                high = recalled[:, 2 * d :].astype(BF)
                r_ref[s, h, part, : 2 * d] = recalled[:, : 2 * d].astype(BF)
                r_ref[s, h, part, 2 * d : 3 * d] = high
                r_ref[s, h, part, 3 * d :] = (recalled[:, 2 * d :] - high.astype(F32)).astype(BF)
                cross = jnp.concatenate([zero, zero, products[:, d:]], axis=1)
                moment = eta * (keep * moment) - dot(products[:, :d].astype(BF), held_low) + cross
                state[s, h] = (stay * held + moment, moment)
    late = 1 - (me & 1)
    for h in range(heads):
        maps = [jnp.concatenate(state[s, h], axis=0) for s in range(2)]
        earlier, later = ordered(me & 1, maps[0], maps[1])
        low = earlier.astype(BF)
        total = compose(later, low)
        group_ref[h] = total.astype(BF)
        if is_last:
            level = [others[g][h] for g in range(groups - 1)] + [total]
            bit = 2
            while len(level) > 1:
                joined = []
                for i in range(0, len(level), 2):
                    earlier, later = ordered(me & bit, level[i].astype(F32), level[i + 1].astype(F32))
                    joined.append(compose(later, earlier))
                level = joined
                bit *= 2
            total_refs[0][h] = level[0].astype(BF)
        recalled = r_ref[late, h]
        folded = dot(recalled[:, : 2 * d], low)
        shift = folded[:, 2 * d :] + recalled[:, 2 * d : 3 * d].astype(F32) + recalled[:, 3 * d :].astype(F32)
        high = shift.astype(BF)
        r_ref[late, h, :, : 2 * d] = folded[:, : 2 * d].astype(BF)
        r_ref[late, h, :, 2 * d : 3 * d] = high
        r_ref[late, h, :, 3 * d :] = (shift - high.astype(F32)).astype(BF)
    copies.append(pltpu.make_async_copy(r_ref, store_ref.at[pl.ds(rel, 2)], sem.at[packs]))
    copies[-1].start()
    for one in copies:
        one.wait()


def pair_call(meta, flat, table, xs, gain, w, gates, initial, rel, before, is_last, counts):
    total_blocks = sum(counts)
    heads, d = gates.shape[0], gates.shape[1]
    parts = [len(x) for x in xs]
    rows = sum(x.shape[0] for x in xs[0])
    blocks = rows // SPAN
    groups = len(before) + 1
    extra = [b["map"] for b in before] + [b["kv"][0] for b in before] if is_last else []
    hbm = pl.BlockSpec(memory_space=pltpu.HBM)
    aliases = {}
    extra_specs = [vmem()] * len(extra)
    if rel > 0:
        aliases = {3 + sum(parts) + 4 + len(extra): 0}
        extra.append(before[-1]["r"])
        extra_specs.append(hbm)
    row = heads * 2 * d
    shapes = [
        jax.ShapeDtypeStruct((STORE_BYTES // (heads * rows * 8 * d), heads, rows, 4 * d), BF),
        jax.ShapeDtypeStruct((heads, 2 * d, 3 * d), BF),
    ]
    counts = counts if is_last else (2 * blocks,)
    shapes += [jax.ShapeDtypeStruct((n, SPAN, row), BF) for n in counts]
    specs = [hbm, vmem()] + [hbm] * len(counts)
    if is_last:
        shapes.append(jax.ShapeDtypeStruct((heads, 2 * d, 3 * d), BF))
        specs.append(vmem())
    if rel == 0:
        shapes.append(jax.ShapeDtypeStruct((total_blocks,), jnp.int32))
        specs.append(smem())
    out = pl.pallas_call(
        functools.partial(pair_kernel, heads, d, blocks, rel, is_last, groups, parts, len(counts)),
        out_shape=shapes,
        grid=(1,),
        in_specs=[smem()] * 3
        + [vmem()] * (sum(parts) + 4)
        + extra_specs,
        out_specs=specs,
        input_output_aliases=aliases,
        scratch_shapes=[
            pltpu.VMEM((sum(counts), SPAN, row), BF),
            pltpu.VMEM((2, heads, rows, 4 * d), BF),
            pltpu.SemaphoreType.DMA((len(counts) + 1,)),
        ],
        compiler_params=params(),
        cost_estimate=cost(2.5e9, 8e6),
        name="pair_last" if is_last else "pair_first",
    )(meta, flat, table, *xs[0], *xs[1], gain, w, gates, initial, *extra)
    return {"r": out[0], "map": out[1], "kv": list(out[2 : 2 + len(counts)]), "total": out[-1]}


def join_kernel(heads, d, meta_ref, own_ref, got_ref, a_ref, b_ref):
    for h in range(heads):
        earlier, later = ordered(meta_ref[1] & 1, own_ref[h].astype(F32), got_ref[h].astype(F32))
        joined = compose(later, earlier).astype(BF)
        a_ref[h] = joined[:, : 2 * d]
        b_ref[h] = joined[:, 2 * d :]


def join(meta, own, got):
    heads, rows, _ = own.shape
    d = rows // 2
    return pl.pallas_call(
        functools.partial(join_kernel, heads, d),
        out_shape=[jax.ShapeDtypeStruct((heads, rows, n), BF) for n in (rows, d)],
        in_specs=[smem(), vmem(), vmem()],
        out_specs=[vmem()] * 2,
        compiler_params=params(),
        cost_estimate=cost(1e8, 1.2e6),
        name="join",
    )(meta, own, got)


def step_kernel(heads, a_ref, b_ref, state_ref, out_ref):
    for h in range(heads):
        out_ref[h] = (dot(a_ref[h], state_ref[h]) + b_ref[h].astype(F32)).astype(BF)


def step(a, b, state):
    return pl.pallas_call(
        functools.partial(step_kernel, a.shape[0]),
        out_shape=jax.ShapeDtypeStruct(b.shape, BF),
        in_specs=[vmem()] * 3,
        out_specs=vmem(),
        compiler_params=params(),
        cost_estimate=cost(1e8, 6e5),
        name="step",
    )(a, b, state)


def recall_kernel(heads, d, groups, *refs):
    meta_ref, got_ref, state_ref = refs[:3]
    map_refs, store_ref = refs[3 : 3 + groups], refs[3 + groups]
    out_refs, (r_ref, sem) = refs[4 + groups : -2], refs[-2:]
    shards = 2 * groups
    loads = [pltpu.make_async_copy(store_ref.at[r], r_ref.at[r], sem.at[r]) for r in range(shards)]
    for one in reversed(loads):
        one.start()
    me, odd = meta_ref[0], (meta_ref[1] & 1) != 0
    d2 = 2 * d
    apply = lambda m, e: dot(m[:, :d2], e.astype(BF)) + m[:, d2:].astype(F32)
    entering = []
    for h in range(heads):
        state = state_ref[h].astype(F32)
        state = jnp.where(odd, apply(got_ref[h], state), state)
        levels = [[map_refs[g][h] for g in range(groups)]]
        bit = 2
        while len(levels[-1]) > 2:
            level, joined = levels[-1], []
            for i in range(0, len(level), 2):
                earlier, later = ordered(me & bit, level[i].astype(F32), level[i + 1].astype(F32))
                joined.append(compose(later, earlier).astype(BF))
            levels.append(joined)
            bit *= 2
        states = [state]
        for level in reversed(levels):
            spread = []
            for i, one in enumerate(states):
                swap = (me & bit) != 0
                after = apply(jnp.where(swap, level[2 * i + 1], level[2 * i]), one)
                spread += [jnp.where(swap, after, one), jnp.where(swap, one, after)]
            states = spread
            bit //= 2
        entering.append([one.astype(BF) for one in states])
    for r in reversed(range(shards)):
        loads[r].wait()
        for h in range(heads):
            recalled = dot(r_ref[r, h, :, :d2], entering[h][r // 2])
            recalled += r_ref[r, h, :, d2 : 3 * d].astype(F32) + r_ref[r, h, :, 3 * d :].astype(F32)
            out_refs[r][:, h * d : (h + 1) * d] = rms_plain(recalled).astype(BF)


def recall(meta, got, state, pairs):
    groups = len(pairs)
    _, heads, rows, width = pairs[-1]["r"].shape
    d = width // 4
    return pl.pallas_call(
        functools.partial(recall_kernel, heads, d, groups),
        out_shape=[jax.ShapeDtypeStruct((rows, heads * d), BF)] * (2 * groups),
        in_specs=[smem()] + [vmem()] * (2 + groups) + [pl.BlockSpec(memory_space=pltpu.HBM)],
        out_specs=[vmem()] * (2 * groups),
        scratch_shapes=[
            pltpu.VMEM((2 * groups, heads, rows, width), BF),
            pltpu.SemaphoreType.DMA((2 * groups,)),
        ],
        compiler_params=params(),
        cost_estimate=cost(2e8, 3e6),
        name="recall",
    )(meta, got, state, *[p["map"] for p in pairs], pairs[-1]["r"])


def ffn_kernel(shards, tile, *refs):
    sources, out_ref, targets = refs[: 2 * shards + 5], refs[2 * shards + 5], refs[2 * shards + 6 : -3]
    hidden_ref, residual_ref, sem = refs[-3:]
    wg_ref, wu_ref, wd_ref = targets[-3:]
    small = [
        pltpu.make_async_copy(source, target, sem.at[i])
        for i, (source, target) in enumerate(zip(sources[:-3], targets[:-3]))
    ]
    down = pltpu.make_async_copy(sources[-1], wd_ref, sem.at[len(small)])
    columns = []
    for i in range(wg_ref.shape[1] // tile):
        part = pl.ds(i * tile, tile)
        at = len(small) + 1 + 2 * i
        columns.append(
            [
                pltpu.make_async_copy(sources[-3].at[:, part], wg_ref.at[:, part], sem.at[at]),
                pltpu.make_async_copy(sources[-2].at[:, part], wu_ref.at[:, part], sem.at[at + 1]),
            ]
        )
    for one in small + [one for pair in columns for one in pair] + [down]:
        one.start()
    for one in small:
        one.wait()
    x_ref, gain_ref = targets[:2]
    residual = x_ref[...].astype(F32)
    for r in range(shards):
        residual += dot(targets[2 + r][...], targets[2 + shards + r][...])
    residual_ref[...] = residual
    scale = lax.rsqrt(jnp.mean(residual * residual, axis=-1, keepdims=True) + EPS)
    low = (residual * scale * gain_ref[...]).astype(BF)
    for i, pair in enumerate(columns):
        for one in pair:
            one.wait()
        part = slice(i * tile, (i + 1) * tile)
        gate = dot(low, wg_ref[:, part])
        up = dot(low, wu_ref[:, part])
        hidden_ref[:, part] = (gate / (1.0 + jnp.exp(-gate)) * up).astype(BF)
    down.wait()
    out_ref[...] = (residual_ref[...] + dot(hidden_ref[...], wd_ref[...])).astype(BF)


def ffn(x, gain, w_out, pieces, w_gate, w_up, w_down):
    rows, width = x.shape
    hidden = w_gate.shape[1]
    tile = 256
    while hidden % tile:
        tile //= 2
    shards = len(pieces)
    sources = [x, gain, *pieces, *w_out, w_gate, w_up, w_down]
    return pl.pallas_call(
        functools.partial(ffn_kernel, shards, tile),
        out_shape=jax.ShapeDtypeStruct((rows, width), BF),
        in_specs=[pl.BlockSpec(memory_space=pl.ANY)] * len(sources),
        out_specs=vmem(),
        scratch_shapes=[pltpu.VMEM(a.shape, a.dtype) for a in sources]
        + [
            pltpu.VMEM((rows, hidden), BF),
            pltpu.VMEM((rows, width), F32),
            pltpu.SemaphoreType.DMA((2 * shards + 3 + 2 * (hidden // tile),)),
        ],
        compiler_params=params(MOST_VMEM),
        cost_estimate=cost(5e9, 2.2e7),
        name="ffn",
    )(*sources)


def regroup_kernel(plan, *refs):
    sources, targets, (stage, sem_in, sem_out) = refs[: plan.sources], refs[plan.sources : -3], refs[-3:]
    into, out, starts = [], [], []
    at = 0
    for i, source in enumerate(sources):
        starts.append(at)
        into.append(pltpu.make_async_copy(source, stage.at[pl.ds(at, source.shape[0])], sem_in.at[i]))
        at += source.shape[0]
    for target, pieces in zip(targets, plan.targets):
        place = 0
        for which, first, count in pieces:
            out.append(
                pltpu.make_async_copy(
                    stage.at[pl.ds(starts[which] + first, count)], target.at[pl.ds(place, count)], sem_out.at[len(out)]
                )
            )
            place += count
    for one in into:
        one.start()
    for one in into:
        one.wait()
    for one in out:
        one.start()
    for one in out:
        one.wait()


class Plan:
    def __init__(self, sources, targets):
        self.sources, self.targets = sources, targets


def regroup(sources, targets):
    block = sources[0].shape[1:]
    hbm = pl.BlockSpec(memory_space=pltpu.HBM)
    return pl.pallas_call(
        functools.partial(regroup_kernel, Plan(len(sources), targets)),
        out_shape=[jax.ShapeDtypeStruct((sum(c for _, _, c in pieces),) + block, BF) for pieces in targets],
        in_specs=[hbm] * len(sources),
        out_specs=[hbm] * len(targets),
        scratch_shapes=[
            pltpu.VMEM((sum(a.shape[0] for a in sources),) + block, BF),
            pltpu.SemaphoreType.DMA((len(sources),)),
            pltpu.SemaphoreType.DMA((sum(len(pieces) for pieces in targets),)),
        ],
        compiler_params=params(),
        cost_estimate=cost(0, 4e6),
        name="regroup",
    )(*sources)


def place_kernel(slots, rows_ref, *refs):
    sources, (out_ref, stage, sem_in, sem_out) = refs[:-4], refs[-4:]
    into, out = [], []
    for source, held in zip(sources, slots):
        for i in range(source.shape[0]):
            n = held[i]
            into.append(pltpu.make_async_copy(source.at[i], stage.at[n], sem_in.at[n]))
            out.append(pltpu.make_async_copy(stage.at[n], out_ref.at[rows_ref[n]], sem_out.at[n]))
    for one in into:
        one.start()
    for first, second in zip(into, out):
        first.wait()
        second.start()
    for one in out:
        one.wait()


def place(rows, sources, slots):
    anywhere = pl.BlockSpec(memory_space=pl.ANY)
    count = rows.shape[0]
    shape = (count,) + sources[0].shape[1:]
    return pl.pallas_call(
        functools.partial(place_kernel, slots),
        out_shape=jax.ShapeDtypeStruct(shape, sources[0].dtype),
        in_specs=[smem()] + [anywhere] * len(sources),
        out_specs=anywhere,
        scratch_shapes=[
            pltpu.VMEM(shape, sources[0].dtype),
            pltpu.SemaphoreType.DMA((count,)),
            pltpu.SemaphoreType.DMA((count,)),
        ],
        compiler_params=params(MOST_VMEM),
        cost_estimate=cost(0, 4 * sources[0].size * len(sources)),
        name="place",
    )(rows, *sources)


def per_device(
    tokens,
    norm_gain,
    w_qkv,
    w_mem_gates,
    persist_keys,
    persist_values,
    alpha_bias,
    eta_bias,
    w_out,
    ffn_gain,
    w_gate,
    w_up,
    w_down,
    segment_ids,
    block_table,
):
    model_dim = tokens.shape[1]
    heads, d = w_qkv.shape[1], w_mem_gates.shape[2]
    shards = lax.axis_size("head")
    n_seq = lax.axis_size("seq")
    seq_index, head_index = lax.axis_index("seq"), lax.axis_index("head")
    blocks_here = shards * tokens.shape[0] // SPAN
    per_owner = PER_OWNER

    count = tokens.shape[0] // SPAN
    cut = tokens.shape[0] // CUTS
    parts = [tokens[i * cut : (i + 1) * cut] for i in range(CUTS)] if CUTS > 1 else [tokens]
    far = [[exchange(part, "head", 2 * g) for part in parts] for g in range(1, shards // 2)]
    xs = {0: [parts, [exchange(tokens, "head", 1)]]}
    w_core = exchange(w_out, "head", 1)

    int32 = jnp.int32
    half = blocks_here // 2
    parity, place_in_line = seq_index & 1, seq_index >> 1
    id_blocks = segment_ids.reshape(-1, SPAN)[:, 0]
    keep_all = jnp.concatenate([jnp.zeros((1,), F32), (id_blocks[1:] == id_blocks[:-1]).astype(F32)])
    keep = lax.dynamic_slice_in_dim(keep_all, seq_index * blocks_here, blocks_here)
    flat = jnp.concatenate([keep, alpha_bias, eta_bias])
    seq = seq_index.astype(int32)[None]

    meta = jnp.stack([head_index, seq_index]).astype(int32)
    slots = jnp.arange(blocks_here, dtype=int32)
    line = n_seq // 2
    early = list(range(line // 2, line))
    others = list(range(1, line // 2))

    gates = jnp.broadcast_to(
        jnp.transpose(w_mem_gates, (0, 2, 1))[:, :, :, None], (heads, d, 3, d)
    ).reshape(heads, d, 3 * d)
    w = w_qkv.reshape(model_dim, heads * 3 * d)
    gain = norm_gain.reshape(1, -1)
    pkeys = persist_keys.reshape(PERS, heads, d)
    pvalues = persist_values.reshape(PERS, heads, d)
    initial = jnp.einsum("phd,phe->hde", pkeys, pvalues, preferred_element_type=F32) / PERS

    pairs = []
    groups = shards // 2
    for g in range(groups):
        if g > 0:
            far[g - 1], pairs[0]["map"], w_core = lax.optimization_barrier((far[g - 1], pairs[0]["map"], w_core))
            xs[g] = [far[g - 1], [exchange(part, "head", 1) for part in far[g - 1]]]
        pairs.append(pair_call(meta, flat, block_table if g == 0 else pairs[0]["total"], xs[g], gain, w, gates, initial, 2 * g, pairs, g == groups - 1, (half,) + (per_owner,) * line))
    total, block_table, w_out = lax.optimization_barrier((pairs[-1]["total"], block_table, w_out))
    w_outs_far = [exchange(w_out, "head", 2 * g) for g in range(1, groups)]
    got = exchange(total, "seq", 1)

    to_me = (block_table // blocks_here == seq_index).reshape(n_seq, blocks_here)
    earlier = to_me[:, None, :] & (slots[None, None, :] < slots[None, :, None])
    sources = jnp.arange(n_seq, dtype=int32)[:, None]
    arrival = (
        jnp.sum(earlier.astype(int32), axis=2)
        + ((sources & 1) ^ parity ^ 1) * half
        + ((sources >> 1) ^ place_in_line) * per_owner
    )
    landed = (arrival.reshape(1, -1) == slots[:, None]) & to_me.reshape(1, -1)
    rows = jnp.sum(jnp.where(landed, (block_table % blocks_here)[None, :], 0), axis=1).astype(int32)

    cross, home, *same = pairs[-1]["kv"]
    far_same = [exchange(same[m - 1], "seq", 2 * m) for m in early]
    a, b = join(meta, total, got)
    b, cross = lax.optimization_barrier((b, cross))
    cross = exchange(cross, "seq", 1)
    onward = [(i, i + 2) for i in range(n_seq - 2)]
    hops = n_seq // 4
    state = b
    for hop in range(hops):
        state = lax.ppermute(state, "seq", onward)
        if hop == 0:
            state, far_same, w_outs_far = lax.optimization_barrier((state, far_same, w_outs_far))
        if hop < hops - 1:
            state = step(a, b, state)
    w_outs = [w_out, w_core] + [w for one in w_outs_far for w in (one, exchange(one, "head", 1))]
    cut = lambda m: (0, m * per_owner, per_owner)
    regrouped = regroup(
        [cross] + [same[m - 1] for m in others],
        [[(1 + i, 0, per_owner), cut(m)] for i, m in enumerate(others)] + [[cut(m)] for m in early] + [[cut(0)]],
    )
    regrouped = list(regrouped)
    retrieved = list(recall(meta, got, state, pairs))
    pieces = [retrieved[0]] + [exchange(retrieved[i], "head", i) for i in range(1, shards)]
    pieces[1], regrouped = lax.optimization_barrier((pieces[1], regrouped))
    arrived = [exchange(one, "seq", 2 * m) for one, m in zip(regrouped, others + early)]
    mixed = ffn(tokens, ffn_gain.reshape(1, -1), w_outs, pieces, w_gate, w_up, w_down)
    held = [regrouped[-1], home] + far_same + arrived
    mixed, held = lax.optimization_barrier((mixed, held))
    of = lambda e, m: [e * half + m * per_owner + i for i in range(per_owner)]
    taken = [of(0, 0), of(1, 0)] + [of(1, m) for m in early]
    taken += [of(1, m) + of(0, m) for m in others] + [of(0, m) for m in early]
    return mixed, place(rows, held, taken)


def solution(mesh):
    return jax.shard_map(
        per_device,
        mesh=mesh,
        in_specs=(
            P(("seq", "head"), None),
            P(),
            P(None, "head", None),
            P("head", None, None),
            P(None, "head"),
            P(None, "head"),
            P("head"),
            P("head"),
            P("head", None),
            P(),
            P(),
            P(),
            P(),
            P(),
            P(),
        ),
        out_specs=(P(("seq", "head"), None), P("seq", None, "head")),
        check_vma=False,
    )
```

```python
import functools

import jax
import jax.numpy as jnp
from jax import lax
from jax.experimental import pallas as pl
from jax.experimental.pallas import tpu as pltpu
from jax.sharding import PartitionSpec as P

PERS = 16
PER_OWNER = 2
SPAN = 64
EPS = 1e-05
TINY = 1e-06
BF = jnp.bfloat16
F32 = jnp.float32
SCALE = 0.001
VMEM_LIMIT = 12 * 1024 * 1024
MOST_VMEM = 60 * 1024 * 1024
STORE_BYTES = 56 * 1024 * 1024
CUTS = 1


def dot(a, b):
    return jnp.dot(a, b, preferred_element_type=F32)


def vmem():
    return pl.BlockSpec(memory_space=pltpu.VMEM)


def smem():
    return pl.BlockSpec(memory_space=pltpu.SMEM)


def loaded(shape):
    return pl.BlockSpec(shape, lambda i: (0,) * len(shape))


def exchange(value, axis, bit):
    count = lax.axis_size(axis)
    return lax.ppermute(value, axis, [(i, i ^ bit) for i in range(count)])


def params(limit=VMEM_LIMIT):
    return pltpu.CompilerParams(vmem_limit_bytes=limit)


def cost(flops, size):
    return pl.CostEstimate(flops=int(flops * SCALE), bytes_accessed=int(size * SCALE), transcendentals=0)


def compose(later, earlier):
    d = later.shape[0] // 2
    joined = dot(later[:, : 2 * d].astype(BF), earlier.astype(BF))
    shift = joined[:, 2 * d :] + later[:, 2 * d :].astype(F32)
    return jnp.concatenate([joined[:, : 2 * d], shift], axis=1)


def ordered(flag, one, other):
    swap = flag != 0
    return jnp.where(swap, other, one), jnp.where(swap, one, other)


def rms_plain(values):
    return values * lax.rsqrt(jnp.mean(values * values, axis=-1, keepdims=True) + TINY)


def pair_kernel(heads, d, blocks, rel, is_last, groups, parts, packs, *refs):
    refs = list(refs)
    meta_ref, flat_ref, slot_ref = refs[:3]
    refs = refs[3:]
    x_refs = [refs[: parts[0]], refs[parts[0] : sum(parts)]]
    refs = refs[sum(parts) :]
    gain_ref, w_ref, gates_ref, start_ref = refs[:4]
    others = refs[4 : 4 + groups - 1] if is_last else []
    kv_before = refs[4 + len(others) : 4 + 2 * len(others)]
    outs = refs[4 + 2 * len(others) + (rel > 0) :]
    store_ref, group_ref = outs[:2]
    kv_outs = outs[2 : 2 + packs]
    total_refs = outs[2 + packs : -3]
    kv_ref, r_ref, sem = outs[-3:]
    bias = flat_ref.shape[0] - 2 * heads
    me = meta_ref[0]
    if rel == 0:
        table_ref, (slot_out,) = slot_ref, total_refs
        here, total_blocks = meta_ref[1], slot_out.shape[0]
        owners = [lax.div(table_ref[here * total_blocks + c], total_blocks) for c in range(total_blocks)]
        for c, owner in enumerate(owners):
            rank = sum([jnp.where(owners[e] == owner, 1, 0) for e in range(c)], jnp.int32(0))
            place = lax.shift_right_logical(owner, 1) ^ lax.shift_right_logical(here, 1)
            cross = (owner & 1) ^ (here & 1)
            slot_out[c] = (1 - cross) * (total_blocks // 2) + place * PER_OWNER + rank
    if is_last:
        for g, source in enumerate(kv_before):
            for i in range(2 * blocks):
                kv_ref[slot_ref[(me ^ (2 * g + i // blocks)) * blocks + i % blocks]] = source[i]
    gain = gain_ref[...]
    w = w_ref[...]
    kept = {}
    for s in range(2):
        x = jnp.concatenate([ref[...] for ref in x_refs[s]], axis=0).astype(F32)
        scale = lax.rsqrt(jnp.mean(x * x, axis=-1, keepdims=True) + EPS)
        projected = dot((x * scale * gain).astype(BF), w)
        base = (me ^ (rel + s)) * blocks
        for h in range(heads):
            q = projected[:, 3 * d * h : 3 * d * h + d]
            k = projected[:, 3 * d * h + d : 3 * d * h + 2 * d]
            v = projected[:, 3 * d * h + 2 * d : 3 * d * h + 3 * d]
            q = rms_plain(q) * d**-0.5
            k = rms_plain(k) * d**-0.5
            kb, vb = k.astype(BF), v.astype(BF)
            logits = dot(vb, gates_ref[h])
            theta = jax.nn.sigmoid(logits[:, :d]) * (1.0 / SPAN)
            weighted = (theta * k).astype(BF)
            both = jnp.concatenate([kb, vb], axis=1)
            items = []
            for c in range(blocks):
                part = slice(c * SPAN, (c + 1) * SPAN)
                where = slot_ref[base + c] if is_last else s * blocks + c
                kv_ref[where, :, 2 * d * h : 2 * d * (h + 1)] = both[part]
                products = lax.dot_general(
                    weighted[part], both[part], (((0,), (0,)), ((), ())), preferred_element_type=F32
                )
                alpha = jax.nn.sigmoid(jnp.mean(logits[part, d : 2 * d], axis=0, keepdims=True) + flat_ref[bias + h])
                eta = jax.nn.sigmoid(
                    jnp.mean(logits[part, 2 * d :], axis=0, keepdims=True) + flat_ref[bias + heads + h]
                )
                widen = lambda row: jnp.concatenate([row, row, row], axis=1)
                items.append((products, widen(1.0 - alpha), widen(eta), q[part].astype(BF), flat_ref[base + c]))
            kept[s, h] = items
    copies, at = [], 0
    for target in kv_outs:
        count = target.shape[0]
        copies.append(pltpu.make_async_copy(kv_ref.at[pl.ds(at, count)], target, sem.at[len(copies)]))
        at += count
    for one in copies:
        one.start()
    zero = jnp.zeros((d, d), F32)
    row = lax.broadcasted_iota(jnp.int32, (d, d), 0)
    column = lax.broadcasted_iota(jnp.int32, (d, d), 1)
    eye = jnp.where(row == column, 1.0, 0.0).astype(F32)
    state = {}
    starts = []
    for h in range(heads):
        first = start_ref[h]
        starts.append(jnp.concatenate([zero, zero, first], axis=1))
    for key in kept:
        state[key] = (jnp.concatenate([eye, zero, zero], axis=1), jnp.concatenate([zero, eye, zero], axis=1))
    for c in range(blocks):
        for s in range(2):
            for h in range(heads):
                products, stay, eta, q, keep = kept[s, h][c]
                memory, moment = state[s, h]
                held = keep * memory + (1.0 - keep) * starts[h]
                held_low = held.astype(BF)
                recalled = dot(q, held_low)
                part = slice(c * SPAN, (c + 1) * SPAN)
                high = recalled[:, 2 * d :].astype(BF)
                r_ref[s, h, part, : 2 * d] = recalled[:, : 2 * d].astype(BF)
                r_ref[s, h, part, 2 * d : 3 * d] = high
                r_ref[s, h, part, 3 * d :] = (recalled[:, 2 * d :] - high.astype(F32)).astype(BF)
                cross = jnp.concatenate([zero, zero, products[:, d:]], axis=1)
                moment = eta * (keep * moment) - dot(products[:, :d].astype(BF), held_low) + cross
                state[s, h] = (stay * held + moment, moment)
    late = 1 - (me & 1)
    for h in range(heads):
        maps = [jnp.concatenate(state[s, h], axis=0) for s in range(2)]
        earlier, later = ordered(me & 1, maps[0], maps[1])
        low = earlier.astype(BF)
        total = compose(later, low)
        group_ref[h] = total.astype(BF)
        if is_last:
            level = [others[g][h] for g in range(groups - 1)] + [total]
            bit = 2
            while len(level) > 1:
                joined = []
                for i in range(0, len(level), 2):
                    earlier, later = ordered(me & bit, level[i].astype(F32), level[i + 1].astype(F32))
                    joined.append(compose(later, earlier))
                level = joined
                bit *= 2
            total_refs[0][h] = level[0].astype(BF)
        recalled = r_ref[late, h]
        folded = dot(recalled[:, : 2 * d], low)
        shift = folded[:, 2 * d :] + recalled[:, 2 * d : 3 * d].astype(F32) + recalled[:, 3 * d :].astype(F32)
        high = shift.astype(BF)
        r_ref[late, h, :, : 2 * d] = folded[:, : 2 * d].astype(BF)
        r_ref[late, h, :, 2 * d : 3 * d] = high
        r_ref[late, h, :, 3 * d :] = (shift - high.astype(F32)).astype(BF)
    copies.append(pltpu.make_async_copy(r_ref, store_ref.at[pl.ds(rel, 2)], sem.at[packs]))
    copies[-1].start()
    for one in copies:
        one.wait()


def pair_call(meta, flat, table, xs, gain, w, gates, initial, rel, before, is_last, counts):
    total_blocks = sum(counts)
    heads, d = gates.shape[0], gates.shape[1]
    parts = [len(x) for x in xs]
    rows = sum(x.shape[0] for x in xs[0])
    blocks = rows // SPAN
    groups = len(before) + 1
    extra = [b["map"] for b in before] + [b["kv"][0] for b in before] if is_last else []
    hbm = pl.BlockSpec(memory_space=pltpu.HBM)
    aliases = {}
    extra_specs = [vmem()] * len(extra)
    if rel > 0:
        aliases = {3 + sum(parts) + 4 + len(extra): 0}
        extra.append(before[-1]["r"])
        extra_specs.append(hbm)
    row = heads * 2 * d
    shapes = [
        jax.ShapeDtypeStruct((STORE_BYTES // (heads * rows * 8 * d), heads, rows, 4 * d), BF),
        jax.ShapeDtypeStruct((heads, 2 * d, 3 * d), BF),
    ]
    counts = counts if is_last else (2 * blocks,)
    shapes += [jax.ShapeDtypeStruct((n, SPAN, row), BF) for n in counts]
    specs = [hbm, vmem()] + [hbm] * len(counts)
    if is_last:
        shapes.append(jax.ShapeDtypeStruct((heads, 2 * d, 3 * d), BF))
        specs.append(vmem())
    if rel == 0:
        shapes.append(jax.ShapeDtypeStruct((total_blocks,), jnp.int32))
        specs.append(smem())
    out = pl.pallas_call(
        functools.partial(pair_kernel, heads, d, blocks, rel, is_last, groups, parts, len(counts)),
        out_shape=shapes,
        grid=(1,),
        in_specs=[smem()] * 3
        + [vmem()] * (sum(parts) + 4)
        + extra_specs,
        out_specs=specs,
        input_output_aliases=aliases,
        scratch_shapes=[
            pltpu.VMEM((sum(counts), SPAN, row), BF),
            pltpu.VMEM((2, heads, rows, 4 * d), BF),
            pltpu.SemaphoreType.DMA((len(counts) + 1,)),
        ],
        compiler_params=params(),
        cost_estimate=cost(2.5e9, 8e6),
        name="pair_last" if is_last else "pair_first",
    )(meta, flat, table, *xs[0], *xs[1], gain, w, gates, initial, *extra)
    return {"r": out[0], "map": out[1], "kv": list(out[2 : 2 + len(counts)]), "total": out[-1]}


def join_kernel(heads, d, meta_ref, own_ref, got_ref, a_ref, b_ref):
    for h in range(heads):
        earlier, later = ordered(meta_ref[1] & 1, own_ref[h].astype(F32), got_ref[h].astype(F32))
        joined = compose(later, earlier).astype(BF)
        a_ref[h] = joined[:, : 2 * d]
        b_ref[h] = joined[:, 2 * d :]


def join(meta, own, got):
    heads, rows, _ = own.shape
    d = rows // 2
    return pl.pallas_call(
        functools.partial(join_kernel, heads, d),
        out_shape=[jax.ShapeDtypeStruct((heads, rows, n), BF) for n in (rows, d)],
        in_specs=[smem(), vmem(), vmem()],
        out_specs=[vmem()] * 2,
        compiler_params=params(),
        cost_estimate=cost(1e8, 1.2e6),
        name="join",
    )(meta, own, got)


def step_kernel(heads, a_ref, b_ref, state_ref, out_ref):
    for h in range(heads):
        out_ref[h] = (dot(a_ref[h], state_ref[h]) + b_ref[h].astype(F32)).astype(BF)


def step(a, b, state):
    return pl.pallas_call(
        functools.partial(step_kernel, a.shape[0]),
        out_shape=jax.ShapeDtypeStruct(b.shape, BF),
        in_specs=[vmem()] * 3,
        out_specs=vmem(),
        compiler_params=params(),
        cost_estimate=cost(1e8, 6e5),
        name="step",
    )(a, b, state)


def recall_kernel(heads, d, groups, *refs):
    meta_ref, got_ref, state_ref = refs[:3]
    map_refs, store_ref = refs[3 : 3 + groups], refs[3 + groups]
    out_refs, (r_ref, sem) = refs[4 + groups : -2], refs[-2:]
    shards = 2 * groups
    loads = [pltpu.make_async_copy(store_ref.at[r], r_ref.at[r], sem.at[r]) for r in range(shards)]
    for one in reversed(loads):
        one.start()
    me, odd = meta_ref[0], (meta_ref[1] & 1) != 0
    d2 = 2 * d
    apply = lambda m, e: dot(m[:, :d2], e.astype(BF)) + m[:, d2:].astype(F32)
    entering = []
    for h in range(heads):
        state = state_ref[h].astype(F32)
        state = jnp.where(odd, apply(got_ref[h], state), state)
        levels = [[map_refs[g][h] for g in range(groups)]]
        bit = 2
        while len(levels[-1]) > 2:
            level, joined = levels[-1], []
            for i in range(0, len(level), 2):
                earlier, later = ordered(me & bit, level[i].astype(F32), level[i + 1].astype(F32))
                joined.append(compose(later, earlier).astype(BF))
            levels.append(joined)
            bit *= 2
        states = [state]
        for level in reversed(levels):
            spread = []
            for i, one in enumerate(states):
                swap = (me & bit) != 0
                after = apply(jnp.where(swap, level[2 * i + 1], level[2 * i]), one)
                spread += [jnp.where(swap, after, one), jnp.where(swap, one, after)]
            states = spread
            bit //= 2
        entering.append([one.astype(BF) for one in states])
    for r in reversed(range(shards)):
        loads[r].wait()
        for h in range(heads):
            recalled = dot(r_ref[r, h, :, :d2], entering[h][r // 2])
            recalled += r_ref[r, h, :, d2 : 3 * d].astype(F32) + r_ref[r, h, :, 3 * d :].astype(F32)
            out_refs[r][:, h * d : (h + 1) * d] = rms_plain(recalled).astype(BF)


def recall(meta, got, state, pairs):
    groups = len(pairs)
    _, heads, rows, width = pairs[-1]["r"].shape
    d = width // 4
    return pl.pallas_call(
        functools.partial(recall_kernel, heads, d, groups),
        out_shape=[jax.ShapeDtypeStruct((rows, heads * d), BF)] * (2 * groups),
        in_specs=[smem()] + [vmem()] * (2 + groups) + [pl.BlockSpec(memory_space=pltpu.HBM)],
        out_specs=[vmem()] * (2 * groups),
        scratch_shapes=[
            pltpu.VMEM((2 * groups, heads, rows, width), BF),
            pltpu.SemaphoreType.DMA((2 * groups,)),
        ],
        compiler_params=params(),
        cost_estimate=cost(2e8, 3e6),
        name="recall",
    )(meta, got, state, *[p["map"] for p in pairs], pairs[-1]["r"])


def ffn_kernel(shards, tile, *refs):
    sources, out_ref, targets = refs[: 2 * shards + 5], refs[2 * shards + 5], refs[2 * shards + 6 : -3]
    hidden_ref, residual_ref, sem = refs[-3:]
    wg_ref, wu_ref, wd_ref = targets[-3:]
    small = [
        pltpu.make_async_copy(source, target, sem.at[i])
        for i, (source, target) in enumerate(zip(sources[:-3], targets[:-3]))
    ]
    down = pltpu.make_async_copy(sources[-1], wd_ref, sem.at[len(small)])
    columns = []
    for i in range(wg_ref.shape[1] // tile):
        part = pl.ds(i * tile, tile)
        at = len(small) + 1 + 2 * i
        columns.append(
            [
                pltpu.make_async_copy(sources[-3].at[:, part], wg_ref.at[:, part], sem.at[at]),
                pltpu.make_async_copy(sources[-2].at[:, part], wu_ref.at[:, part], sem.at[at + 1]),
            ]
        )
    for one in small + [one for pair in columns for one in pair] + [down]:
        one.start()
    for one in small:
        one.wait()
    x_ref, gain_ref = targets[:2]
    residual = x_ref[...].astype(F32)
    for r in range(shards):
        residual += dot(targets[2 + r][...], targets[2 + shards + r][...])
    residual_ref[...] = residual
    scale = lax.rsqrt(jnp.mean(residual * residual, axis=-1, keepdims=True) + EPS)
    low = (residual * scale * gain_ref[...]).astype(BF)
    for i, pair in enumerate(columns):
        for one in pair:
            one.wait()
        part = slice(i * tile, (i + 1) * tile)
        gate = dot(low, wg_ref[:, part])
        up = dot(low, wu_ref[:, part])
        hidden_ref[:, part] = (gate / (1.0 + jnp.exp(-gate)) * up).astype(BF)
    down.wait()
    out_ref[...] = (residual_ref[...] + dot(hidden_ref[...], wd_ref[...])).astype(BF)


def ffn(x, gain, w_out, pieces, w_gate, w_up, w_down):
    rows, width = x.shape
    hidden = w_gate.shape[1]
    tile = 256
    while hidden % tile:
        tile //= 2
    shards = len(pieces)
    sources = [x, gain, *pieces, *w_out, w_gate, w_up, w_down]
    return pl.pallas_call(
        functools.partial(ffn_kernel, shards, tile),
        out_shape=jax.ShapeDtypeStruct((rows, width), BF),
        in_specs=[pl.BlockSpec(memory_space=pl.ANY)] * len(sources),
        out_specs=vmem(),
        scratch_shapes=[pltpu.VMEM(a.shape, a.dtype) for a in sources]
        + [
            pltpu.VMEM((rows, hidden), BF),
            pltpu.VMEM((rows, width), F32),
            pltpu.SemaphoreType.DMA((2 * shards + 3 + 2 * (hidden // tile),)),
        ],
        compiler_params=params(MOST_VMEM),
        cost_estimate=cost(5e9, 2.2e7),
        name="ffn",
    )(*sources)


def regroup_kernel(plan, *refs):
    sources, targets, (stage, sem_in, sem_out) = refs[: plan.sources], refs[plan.sources : -3], refs[-3:]
    into, out, starts = [], [], []
    at = 0
    for i, source in enumerate(sources):
        starts.append(at)
        into.append(pltpu.make_async_copy(source, stage.at[pl.ds(at, source.shape[0])], sem_in.at[i]))
        at += source.shape[0]
    for target, pieces in zip(targets, plan.targets):
        place = 0
        for which, first, count in pieces:
            out.append(
                pltpu.make_async_copy(
                    stage.at[pl.ds(starts[which] + first, count)], target.at[pl.ds(place, count)], sem_out.at[len(out)]
                )
            )
            place += count
    for one in into:
        one.start()
    for one in into:
        one.wait()
    for one in out:
        one.start()
    for one in out:
        one.wait()


class Plan:
    def __init__(self, sources, targets):
        self.sources, self.targets = sources, targets


def regroup(sources, targets):
    block = sources[0].shape[1:]
    hbm = pl.BlockSpec(memory_space=pltpu.HBM)
    return pl.pallas_call(
        functools.partial(regroup_kernel, Plan(len(sources), targets)),
        out_shape=[jax.ShapeDtypeStruct((sum(c for _, _, c in pieces),) + block, BF) for pieces in targets],
        in_specs=[hbm] * len(sources),
        out_specs=[hbm] * len(targets),
        scratch_shapes=[
            pltpu.VMEM((sum(a.shape[0] for a in sources),) + block, BF),
            pltpu.SemaphoreType.DMA((len(sources),)),
            pltpu.SemaphoreType.DMA((sum(len(pieces) for pieces in targets),)),
        ],
        compiler_params=params(),
        cost_estimate=cost(0, 4e6),
        name="regroup",
    )(*sources)


def place_kernel(slots, rows_ref, *refs):
    sources, (out_ref, stage, sem_in, sem_out) = refs[:-4], refs[-4:]
    into, out = [], []
    for source, held in zip(sources, slots):
        for i, n in enumerate(held):
            into.append(pltpu.make_async_copy(source.at[i], stage.at[n], sem_in.at[n]))
            out.append(pltpu.make_async_copy(stage.at[n], out_ref.at[rows_ref[n]], sem_out.at[n]))
    for one in into:
        one.start()
    for first, second in zip(into, out):
        first.wait()
        second.start()
    for one in out:
        one.wait()


def place(rows, sources, slots):
    anywhere = pl.BlockSpec(memory_space=pl.ANY)
    count = rows.shape[0]
    shape = (count,) + sources[0].shape[1:]
    return pl.pallas_call(
        functools.partial(place_kernel, slots),
        out_shape=jax.ShapeDtypeStruct(shape, sources[0].dtype),
        in_specs=[smem()] + [anywhere] * len(sources),
        out_specs=anywhere,
        scratch_shapes=[
            pltpu.VMEM(shape, sources[0].dtype),
            pltpu.SemaphoreType.DMA((count,)),
            pltpu.SemaphoreType.DMA((count,)),
        ],
        compiler_params=params(MOST_VMEM),
        cost_estimate=cost(0, 4 * sources[0].size * len(sources)),
        name="place",
    )(rows, *sources)


def per_device(
    tokens,
    norm_gain,
    w_qkv,
    w_mem_gates,
    persist_keys,
    persist_values,
    alpha_bias,
    eta_bias,
    w_out,
    ffn_gain,
    w_gate,
    w_up,
    w_down,
    segment_ids,
    block_table,
):
    model_dim = tokens.shape[1]
    heads, d = w_qkv.shape[1], w_mem_gates.shape[2]
    shards = lax.axis_size("head")
    n_seq = lax.axis_size("seq")
    seq_index, head_index = lax.axis_index("seq"), lax.axis_index("head")
    blocks_here = shards * tokens.shape[0] // SPAN
    per_owner = PER_OWNER

    count = tokens.shape[0] // SPAN
    cut = tokens.shape[0] // CUTS
    parts = [tokens[i * cut : (i + 1) * cut] for i in range(CUTS)] if CUTS > 1 else [tokens]
    far = [[exchange(part, "head", 2 * g) for part in parts] for g in range(1, shards // 2)]
    xs = {0: [parts, [exchange(tokens, "head", 1)]]}
    w_core = exchange(w_out, "head", 1)

    int32 = jnp.int32
    half = blocks_here // 2
    parity, place_in_line = seq_index & 1, seq_index >> 1
    id_blocks = segment_ids.reshape(-1, SPAN)[:, 0]
    keep_all = jnp.concatenate([jnp.zeros((1,), F32), (id_blocks[1:] == id_blocks[:-1]).astype(F32)])
    keep = lax.dynamic_slice_in_dim(keep_all, seq_index * blocks_here, blocks_here)
    flat = jnp.concatenate([keep, alpha_bias, eta_bias])
    seq = seq_index.astype(int32)[None]

    meta = jnp.stack([head_index, seq_index]).astype(int32)
    slots = jnp.arange(blocks_here, dtype=int32)
    line = n_seq // 2
    early = list(range(line // 2, line))
    others = list(range(1, line // 2))

    gates = jnp.broadcast_to(
        jnp.transpose(w_mem_gates, (0, 2, 1))[:, :, :, None], (heads, d, 3, d)
    ).reshape(heads, d, 3 * d)
    w = w_qkv.reshape(model_dim, heads * 3 * d)
    gain = norm_gain.reshape(1, -1)
    pkeys = persist_keys.reshape(PERS, heads, d)
    pvalues = persist_values.reshape(PERS, heads, d)
    initial = jnp.einsum("phd,phe->hde", pkeys, pvalues, preferred_element_type=F32) / PERS

    pairs = []
    groups = shards // 2
    for g in range(groups):
        if g > 0:
            far[g - 1], pairs[0]["map"], w_core = lax.optimization_barrier((far[g - 1], pairs[0]["map"], w_core))
            xs[g] = [far[g - 1], [exchange(part, "head", 1) for part in far[g - 1]]]
        pairs.append(pair_call(meta, flat, block_table if g == 0 else pairs[0]["total"], xs[g], gain, w, gates, initial, 2 * g, pairs, g == groups - 1, (half,) + (per_owner,) * (line // 2) + (half // 2,)))
    total, block_table, w_out = lax.optimization_barrier((pairs[-1]["total"], block_table, w_out))
    w_outs_far = [exchange(w_out, "head", 2 * g) for g in range(1, groups)]
    got = exchange(total, "seq", 1)

    to_me = (block_table // blocks_here == seq_index).reshape(n_seq, blocks_here)
    earlier = to_me[:, None, :] & (slots[None, None, :] < slots[None, :, None])
    sources = jnp.arange(n_seq, dtype=int32)[:, None]
    arrival = (
        jnp.sum(earlier.astype(int32), axis=2)
        + ((sources & 1) ^ parity ^ 1) * half
        + ((sources >> 1) ^ place_in_line) * per_owner
    )
    landed = (arrival.reshape(1, -1) == slots[:, None]) & to_me.reshape(1, -1)
    rows = jnp.sum(jnp.where(landed, (block_table % blocks_here)[None, :], 0), axis=1).astype(int32)

    cross, home, *same, far_same = pairs[-1]["kv"]
    far_same = exchange(far_same, "seq", line)
    a, b = join(meta, total, got)
    b, cross = lax.optimization_barrier((b, cross))
    cross = exchange(cross, "seq", 1)
    onward = [(i, i + 2) for i in range(n_seq - 2)]
    hops = n_seq // 4
    state = b
    for hop in range(hops):
        state = lax.ppermute(state, "seq", onward)
        if hop == 0:
            state, far_same, w_outs_far = lax.optimization_barrier((state, far_same, w_outs_far))
        if hop < hops - 1:
            state = step(a, b, state)
    w_outs = [w_out, w_core] + [w for one in w_outs_far for w in (one, exchange(one, "head", 1))]
    cut = lambda m: (0, m * per_owner, per_owner)
    regrouped = regroup(
        [cross, far_same] + same,
        [[(1 + m, 0, per_owner), cut(m), (1, m * per_owner, per_owner)] for m in others] + [[cut(m)] for m in early] + [[cut(0)]],
    )
    regrouped = list(regrouped)
    retrieved = list(recall(meta, got, state, pairs))
    pieces = [retrieved[0]] + [exchange(retrieved[i], "head", i) for i in range(1, shards)]
    pieces[1], regrouped = lax.optimization_barrier((pieces[1], regrouped))
    arrived = [exchange(one, "seq", 2 * m) for one, m in zip(regrouped, others + early)]
    mixed = ffn(tokens, ffn_gain.reshape(1, -1), w_outs, pieces, w_gate, w_up, w_down)
    held = [regrouped[-1], home, far_same] + arrived
    mixed, held = lax.optimization_barrier((mixed, held))
    of = lambda e, m: [e * half + m * per_owner + i for i in range(per_owner)]
    taken = [of(0, 0), of(1, 0), of(1, line // 2)]
    taken += [of(1, m) + of(0, m) + of(1, m + line // 2) for m in others] + [of(0, m) for m in early]
    return mixed, place(rows, held, taken)


def solution(mesh):
    return jax.shard_map(
        per_device,
        mesh=mesh,
        in_specs=(
            P(("seq", "head"), None),
            P(),
            P(None, "head", None),
            P("head", None, None),
            P(None, "head"),
            P(None, "head"),
            P("head"),
            P("head"),
            P("head", None),
            P(),
            P(),
            P(),
            P(),
            P(),
            P(),
        ),
        out_specs=(P(("seq", "head"), None), P("seq", None, "head")),
        check_vma=False,
    )
```

```python
import functools

import jax
import jax.numpy as jnp
from jax import lax
from jax.experimental import pallas as pl
from jax.experimental.pallas import tpu as pltpu
from jax.sharding import PartitionSpec as P

PERS = 16
PER_OWNER = 2
SPAN = 64
EPS = 1e-05
TINY = 1e-06
BF = jnp.bfloat16
F32 = jnp.float32
SCALE = 0.0
VMEM_LIMIT = 12 * 1024 * 1024
MOST_VMEM = 60 * 1024 * 1024
STORE_BYTES = 56 * 1024 * 1024
CUTS = 1


def dot(a, b):
    return jnp.dot(a, b, preferred_element_type=F32)


def vmem():
    return pl.BlockSpec(memory_space=pltpu.VMEM)


def smem():
    return pl.BlockSpec(memory_space=pltpu.SMEM)


def loaded(shape):
    return pl.BlockSpec(shape, lambda i: (0,) * len(shape))


def exchange(value, axis, bit):
    count = lax.axis_size(axis)
    return lax.ppermute(value, axis, [(i, i ^ bit) for i in range(count)])


def params(limit=VMEM_LIMIT):
    return pltpu.CompilerParams(vmem_limit_bytes=limit)


def cost(flops, size):
    return pl.CostEstimate(flops=int(flops * SCALE), bytes_accessed=int(size * SCALE), transcendentals=0)


def compose(later, earlier):
    d = later.shape[0] // 2
    joined = dot(later[:, : 2 * d].astype(BF), earlier.astype(BF))
    shift = joined[:, 2 * d :] + later[:, 2 * d :].astype(F32)
    return jnp.concatenate([joined[:, : 2 * d], shift], axis=1)


def ordered(flag, one, other):
    swap = flag != 0
    return jnp.where(swap, other, one), jnp.where(swap, one, other)


def rms_plain(values):
    return values * lax.rsqrt(jnp.mean(values * values, axis=-1, keepdims=True) + TINY)


def pair_kernel(heads, d, blocks, rel, is_last, groups, parts, packs, *refs):
    refs = list(refs)
    meta_ref, flat_ref, slot_ref = refs[:3]
    refs = refs[3:]
    x_refs = [refs[: parts[0]], refs[parts[0] : sum(parts)]]
    refs = refs[sum(parts) :]
    gain_ref, w_ref, gates_ref, start_ref = refs[:4]
    others = refs[4 : 4 + groups - 1] if is_last else []
    kv_before = refs[4 + len(others) : 4 + 2 * len(others)]
    outs = refs[4 + 2 * len(others) + (rel > 0) :]
    store_ref, group_ref = outs[:2]
    kv_outs = outs[2 : 2 + packs]
    total_refs = outs[2 + packs : -3]
    kv_ref, r_ref, sem = outs[-3:]
    bias = flat_ref.shape[0] - 2 * heads
    me = meta_ref[0]
    if rel == 0:
        table_ref, (slot_out,) = slot_ref, total_refs
        here, total_blocks = meta_ref[1], slot_out.shape[0]
        owners = [lax.div(table_ref[here * total_blocks + c], total_blocks) for c in range(total_blocks)]
        for c, owner in enumerate(owners):
            rank = sum([jnp.where(owners[e] == owner, 1, 0) for e in range(c)], jnp.int32(0))
            place = lax.shift_right_logical(owner, 1) ^ lax.shift_right_logical(here, 1)
            cross = (owner & 1) ^ (here & 1)
            slot_out[c] = (1 - cross) * (total_blocks // 2) + place * PER_OWNER + rank
    if is_last:
        for g, source in enumerate(kv_before):
            for i in range(2 * blocks):
                kv_ref[slot_ref[(me ^ (2 * g + i // blocks)) * blocks + i % blocks]] = source[i]
    gain = gain_ref[...]
    w = w_ref[...]
    kept = {}
    for s in range(2):
        x = jnp.concatenate([ref[...] for ref in x_refs[s]], axis=0).astype(F32)
        scale = lax.rsqrt(jnp.mean(x * x, axis=-1, keepdims=True) + EPS)
        projected = dot((x * scale * gain).astype(BF), w)
        base = (me ^ (rel + s)) * blocks
        for h in range(heads):
            q = projected[:, 3 * d * h : 3 * d * h + d]
            k = projected[:, 3 * d * h + d : 3 * d * h + 2 * d]
            v = projected[:, 3 * d * h + 2 * d : 3 * d * h + 3 * d]
            q = rms_plain(q) * d**-0.5
            k = rms_plain(k) * d**-0.5
            kb, vb = k.astype(BF), v.astype(BF)
            logits = dot(vb, gates_ref[h])
            theta = jax.nn.sigmoid(logits[:, :d]) * (1.0 / SPAN)
            weighted = (theta * k).astype(BF)
            both = jnp.concatenate([kb, vb], axis=1)
            items = []
            for c in range(blocks):
                part = slice(c * SPAN, (c + 1) * SPAN)
                where = slot_ref[base + c] if is_last else s * blocks + c
                kv_ref[where, :, 2 * d * h : 2 * d * (h + 1)] = both[part]
                products = lax.dot_general(
                    weighted[part], both[part], (((0,), (0,)), ((), ())), preferred_element_type=F32
                )
                alpha = jax.nn.sigmoid(jnp.mean(logits[part, d : 2 * d], axis=0, keepdims=True) + flat_ref[bias + h])
                eta = jax.nn.sigmoid(
                    jnp.mean(logits[part, 2 * d :], axis=0, keepdims=True) + flat_ref[bias + heads + h]
                )
                widen = lambda row: jnp.concatenate([row, row, row], axis=1)
                items.append((products, widen(1.0 - alpha), widen(eta), q[part].astype(BF), flat_ref[base + c]))
            kept[s, h] = items
    copies, at = [], 0
    for target in kv_outs:
        count = target.shape[0]
        copies.append(pltpu.make_async_copy(kv_ref.at[pl.ds(at, count)], target, sem.at[len(copies)]))
        at += count
    for one in copies:
        one.start()
    zero = jnp.zeros((d, d), F32)
    row = lax.broadcasted_iota(jnp.int32, (d, d), 0)
    column = lax.broadcasted_iota(jnp.int32, (d, d), 1)
    eye = jnp.where(row == column, 1.0, 0.0).astype(F32)
    state = {}
    starts = []
    for h in range(heads):
        first = start_ref[h]
        starts.append(jnp.concatenate([zero, zero, first], axis=1))
    for key in kept:
        state[key] = (jnp.concatenate([eye, zero, zero], axis=1), jnp.concatenate([zero, eye, zero], axis=1))
    for c in range(blocks):
        for s in range(2):
            for h in range(heads):
                products, stay, eta, q, keep = kept[s, h][c]
                memory, moment = state[s, h]
                held = keep * memory + (1.0 - keep) * starts[h]
                held_low = held.astype(BF)
                recalled = dot(q, held_low)
                part = slice(c * SPAN, (c + 1) * SPAN)
                high = recalled[:, 2 * d :].astype(BF)
                r_ref[s, h, part, : 2 * d] = recalled[:, : 2 * d].astype(BF)
                r_ref[s, h, part, 2 * d : 3 * d] = high
                r_ref[s, h, part, 3 * d :] = (recalled[:, 2 * d :] - high.astype(F32)).astype(BF)
                cross = jnp.concatenate([zero, zero, products[:, d:]], axis=1)
                moment = eta * (keep * moment) - dot(products[:, :d].astype(BF), held_low) + cross
                state[s, h] = (stay * held + moment, moment)
    late = 1 - (me & 1)
    copies.append(pltpu.make_async_copy(r_ref.at[1 - late], store_ref.at[rel + 1 - late], sem.at[packs]))
    copies[-1].start()
    for h in range(heads):
        maps = [jnp.concatenate(state[s, h], axis=0) for s in range(2)]
        earlier, later = ordered(me & 1, maps[0], maps[1])
        low = earlier.astype(BF)
        total = compose(later, low)
        group_ref[h] = total.astype(BF)
        if is_last:
            level = [others[g][h] for g in range(groups - 1)] + [total]
            bit = 2
            while len(level) > 1:
                joined = []
                for i in range(0, len(level), 2):
                    earlier, later = ordered(me & bit, level[i].astype(F32), level[i + 1].astype(F32))
                    joined.append(compose(later, earlier))
                level = joined
                bit *= 2
            total_refs[0][h] = level[0].astype(BF)
        recalled = r_ref[late, h]
        folded = dot(recalled[:, : 2 * d], low)
        shift = folded[:, 2 * d :] + recalled[:, 2 * d : 3 * d].astype(F32) + recalled[:, 3 * d :].astype(F32)
        high = shift.astype(BF)
        r_ref[late, h, :, : 2 * d] = folded[:, : 2 * d].astype(BF)
        r_ref[late, h, :, 2 * d : 3 * d] = high
        r_ref[late, h, :, 3 * d :] = (shift - high.astype(F32)).astype(BF)
        copies.append(
            pltpu.make_async_copy(r_ref.at[late, h], store_ref.at[rel + late, h], sem.at[packs + 1 + h])
        )
        copies[-1].start()
    for one in copies:
        one.wait()


def pair_call(meta, flat, table, xs, gain, w, gates, initial, rel, before, is_last, counts):
    total_blocks = sum(counts)
    heads, d = gates.shape[0], gates.shape[1]
    parts = [len(x) for x in xs]
    rows = sum(x.shape[0] for x in xs[0])
    blocks = rows // SPAN
    groups = len(before) + 1
    extra = [b["map"] for b in before] + [b["kv"][0] for b in before] if is_last else []
    hbm = pl.BlockSpec(memory_space=pltpu.HBM)
    aliases = {}
    extra_specs = [vmem()] * len(extra)
    if rel > 0:
        aliases = {3 + sum(parts) + 4 + len(extra): 0}
        extra.append(before[-1]["r"])
        extra_specs.append(hbm)
    row = heads * 2 * d
    shapes = [
        jax.ShapeDtypeStruct((STORE_BYTES // (heads * rows * 8 * d), heads, rows, 4 * d), BF),
        jax.ShapeDtypeStruct((heads, 2 * d, 3 * d), BF),
    ]
    counts = counts if is_last else (2 * blocks,)
    shapes += [jax.ShapeDtypeStruct((n, SPAN, row), BF) for n in counts]
    specs = [hbm, vmem()] + [hbm] * len(counts)
    if is_last:
        shapes.append(jax.ShapeDtypeStruct((heads, 2 * d, 3 * d), BF))
        specs.append(vmem())
    if rel == 0:
        shapes.append(jax.ShapeDtypeStruct((total_blocks,), jnp.int32))
        specs.append(smem())
    out = pl.pallas_call(
        functools.partial(pair_kernel, heads, d, blocks, rel, is_last, groups, parts, len(counts)),
        out_shape=shapes,
        grid=(1,),
        in_specs=[smem()] * 3
        + [vmem()] * (sum(parts) + 4)
        + extra_specs,
        out_specs=specs,
        input_output_aliases=aliases,
        scratch_shapes=[
            pltpu.VMEM((sum(counts), SPAN, row), BF),
            pltpu.VMEM((2, heads, rows, 4 * d), BF),
            pltpu.SemaphoreType.DMA((len(counts) + 1 + heads,)),
        ],
        compiler_params=params(),
        cost_estimate=cost(2.5e9, 8e6),
        name="pair_last" if is_last else "pair_first",
    )(meta, flat, table, *xs[0], *xs[1], gain, w, gates, initial, *extra)
    return {"r": out[0], "map": out[1], "kv": list(out[2 : 2 + len(counts)]), "total": out[-1]}


def join_kernel(heads, d, meta_ref, own_ref, got_ref, a_ref, b_ref):
    for h in range(heads):
        earlier, later = ordered(meta_ref[1] & 1, own_ref[h].astype(F32), got_ref[h].astype(F32))
        joined = compose(later, earlier).astype(BF)
        a_ref[h] = joined[:, : 2 * d]
        b_ref[h] = joined[:, 2 * d :]


def join(meta, own, got):
    heads, rows, _ = own.shape
    d = rows // 2
    return pl.pallas_call(
        functools.partial(join_kernel, heads, d),
        out_shape=[jax.ShapeDtypeStruct((heads, rows, n), BF) for n in (rows, d)],
        in_specs=[smem(), vmem(), vmem()],
        out_specs=[vmem()] * 2,
        compiler_params=params(),
        cost_estimate=cost(1e8, 1.2e6),
        name="join",
    )(meta, own, got)


def step_kernel(heads, a_ref, b_ref, state_ref, out_ref):
    for h in range(heads):
        out_ref[h] = (dot(a_ref[h], state_ref[h]) + b_ref[h].astype(F32)).astype(BF)


def step(a, b, state):
    return pl.pallas_call(
        functools.partial(step_kernel, a.shape[0]),
        out_shape=jax.ShapeDtypeStruct(b.shape, BF),
        in_specs=[vmem()] * 3,
        out_specs=vmem(),
        compiler_params=params(),
        cost_estimate=cost(1e8, 6e5),
        name="step",
    )(a, b, state)


def recall_kernel(heads, d, groups, *refs):
    meta_ref, got_ref, state_ref = refs[:3]
    map_refs, store_ref = refs[3 : 3 + groups], refs[3 + groups]
    out_refs, (r_ref, sem) = refs[4 + groups : -2], refs[-2:]
    shards = 2 * groups
    loads = [pltpu.make_async_copy(store_ref.at[r], r_ref.at[r], sem.at[r]) for r in range(shards)]
    for one in reversed(loads):
        one.start()
    me, odd = meta_ref[0], (meta_ref[1] & 1) != 0
    d2 = 2 * d
    apply = lambda m, e: dot(m[:, :d2], e.astype(BF)) + m[:, d2:].astype(F32)
    entering = []
    for h in range(heads):
        state = state_ref[h].astype(F32)
        state = jnp.where(odd, apply(got_ref[h], state), state)
        levels = [[map_refs[g][h] for g in range(groups)]]
        bit = 2
        while len(levels[-1]) > 2:
            level, joined = levels[-1], []
            for i in range(0, len(level), 2):
                earlier, later = ordered(me & bit, level[i].astype(F32), level[i + 1].astype(F32))
                joined.append(compose(later, earlier).astype(BF))
            levels.append(joined)
            bit *= 2
        states = [state]
        for level in reversed(levels):
            spread = []
            for i, one in enumerate(states):
                swap = (me & bit) != 0
                after = apply(jnp.where(swap, level[2 * i + 1], level[2 * i]), one)
                spread += [jnp.where(swap, after, one), jnp.where(swap, one, after)]
            states = spread
            bit //= 2
        entering.append([one.astype(BF) for one in states])
    for r in reversed(range(shards)):
        loads[r].wait()
        for h in range(heads):
            recalled = dot(r_ref[r, h, :, :d2], entering[h][r // 2])
            recalled += r_ref[r, h, :, d2 : 3 * d].astype(F32) + r_ref[r, h, :, 3 * d :].astype(F32)
            out_refs[r][:, h * d : (h + 1) * d] = rms_plain(recalled).astype(BF)


def recall(meta, got, state, pairs):
    groups = len(pairs)
    _, heads, rows, width = pairs[-1]["r"].shape
    d = width // 4
    return pl.pallas_call(
        functools.partial(recall_kernel, heads, d, groups),
        out_shape=[jax.ShapeDtypeStruct((rows, heads * d), BF)] * (2 * groups),
        in_specs=[smem()] + [vmem()] * (2 + groups) + [pl.BlockSpec(memory_space=pltpu.HBM)],
        out_specs=[vmem()] * (2 * groups),
        scratch_shapes=[
            pltpu.VMEM((2 * groups, heads, rows, width), BF),
            pltpu.SemaphoreType.DMA((2 * groups,)),
        ],
        compiler_params=params(),
        cost_estimate=cost(2e8, 3e6),
        name="recall",
    )(meta, got, state, *[p["map"] for p in pairs], pairs[-1]["r"])


def ffn_kernel(shards, tile, *refs):
    sources, out_ref, targets = refs[: 2 * shards + 5], refs[2 * shards + 5], refs[2 * shards + 6 : -3]
    hidden_ref, residual_ref, sem = refs[-3:]
    wg_ref, wu_ref, wd_ref = targets[-3:]
    small = [
        pltpu.make_async_copy(source, target, sem.at[i])
        for i, (source, target) in enumerate(zip(sources[:-3], targets[:-3]))
    ]
    down = pltpu.make_async_copy(sources[-1], wd_ref, sem.at[len(small)])
    columns = []
    for i in range(wg_ref.shape[1] // tile):
        part = pl.ds(i * tile, tile)
        at = len(small) + 1 + 2 * i
        columns.append(
            [
                pltpu.make_async_copy(sources[-3].at[:, part], wg_ref.at[:, part], sem.at[at]),
                pltpu.make_async_copy(sources[-2].at[:, part], wu_ref.at[:, part], sem.at[at + 1]),
            ]
        )
    for one in small + [one for pair in columns for one in pair] + [down]:
        one.start()
    for one in small:
        one.wait()
    x_ref, gain_ref = targets[:2]
    residual = x_ref[...].astype(F32)
    for r in range(shards):
        residual += dot(targets[2 + r][...], targets[2 + shards + r][...])
    residual_ref[...] = residual
    scale = lax.rsqrt(jnp.mean(residual * residual, axis=-1, keepdims=True) + EPS)
    low = (residual * scale * gain_ref[...]).astype(BF)
    for i, pair in enumerate(columns):
        for one in pair:
            one.wait()
        part = slice(i * tile, (i + 1) * tile)
        gate = dot(low, wg_ref[:, part])
        up = dot(low, wu_ref[:, part])
        hidden_ref[:, part] = (gate / (1.0 + jnp.exp(-gate)) * up).astype(BF)
    down.wait()
    out_ref[...] = (residual_ref[...] + dot(hidden_ref[...], wd_ref[...])).astype(BF)


def ffn(x, gain, w_out, pieces, w_gate, w_up, w_down):
    rows, width = x.shape
    hidden = w_gate.shape[1]
    tile = 256
    while hidden % tile:
        tile //= 2
    shards = len(pieces)
    sources = [x, gain, *pieces, *w_out, w_gate, w_up, w_down]
    return pl.pallas_call(
        functools.partial(ffn_kernel, shards, tile),
        out_shape=jax.ShapeDtypeStruct((rows, width), BF),
        in_specs=[pl.BlockSpec(memory_space=pl.ANY)] * len(sources),
        out_specs=vmem(),
        scratch_shapes=[pltpu.VMEM(a.shape, a.dtype) for a in sources]
        + [
            pltpu.VMEM((rows, hidden), BF),
            pltpu.VMEM((rows, width), F32),
            pltpu.SemaphoreType.DMA((2 * shards + 3 + 2 * (hidden // tile),)),
        ],
        compiler_params=params(MOST_VMEM),
        cost_estimate=cost(5e9, 2.2e7),
        name="ffn",
    )(*sources)


def regroup_kernel(plan, *refs):
    sources, targets, (stage, sem_in, sem_out) = refs[: plan.sources], refs[plan.sources : -3], refs[-3:]
    into, out, starts = [], [], []
    at = 0
    for i, source in enumerate(sources):
        starts.append(at)
        into.append(pltpu.make_async_copy(source, stage.at[pl.ds(at, source.shape[0])], sem_in.at[i]))
        at += source.shape[0]
    for target, pieces in zip(targets, plan.targets):
        place = 0
        for which, first, count in pieces:
            out.append(
                pltpu.make_async_copy(
                    stage.at[pl.ds(starts[which] + first, count)], target.at[pl.ds(place, count)], sem_out.at[len(out)]
                )
            )
            place += count
    for one in into:
        one.start()
    for one in into:
        one.wait()
    for one in out:
        one.start()
    for one in out:
        one.wait()


class Plan:
    def __init__(self, sources, targets):
        self.sources, self.targets = sources, targets


def regroup(sources, targets):
    block = sources[0].shape[1:]
    hbm = pl.BlockSpec(memory_space=pltpu.HBM)
    return pl.pallas_call(
        functools.partial(regroup_kernel, Plan(len(sources), targets)),
        out_shape=[jax.ShapeDtypeStruct((sum(c for _, _, c in pieces),) + block, BF) for pieces in targets],
        in_specs=[hbm] * len(sources),
        out_specs=[hbm] * len(targets),
        scratch_shapes=[
            pltpu.VMEM((sum(a.shape[0] for a in sources),) + block, BF),
            pltpu.SemaphoreType.DMA((len(sources),)),
            pltpu.SemaphoreType.DMA((sum(len(pieces) for pieces in targets),)),
        ],
        compiler_params=params(),
        cost_estimate=cost(0, 4e6),
        name="regroup",
    )(*sources)


def place_kernel(slots, rows_ref, *refs):
    sources, (out_ref, stage, sem_in, sem_out) = refs[:-4], refs[-4:]
    into, out = [], []
    for source, held in zip(sources, slots):
        for i, n in enumerate(held):
            into.append(pltpu.make_async_copy(source.at[i], stage.at[n], sem_in.at[n]))
            out.append(pltpu.make_async_copy(stage.at[n], out_ref.at[rows_ref[n]], sem_out.at[n]))
    for one in into:
        one.start()
    for first, second in zip(into, out):
        first.wait()
        second.start()
    for one in out:
        one.wait()


def place(rows, sources, slots):
    anywhere = pl.BlockSpec(memory_space=pl.ANY)
    count = rows.shape[0]
    shape = (count,) + sources[0].shape[1:]
    return pl.pallas_call(
        functools.partial(place_kernel, slots),
        out_shape=jax.ShapeDtypeStruct(shape, sources[0].dtype),
        in_specs=[smem()] + [anywhere] * len(sources),
        out_specs=anywhere,
        scratch_shapes=[
            pltpu.VMEM(shape, sources[0].dtype),
            pltpu.SemaphoreType.DMA((count,)),
            pltpu.SemaphoreType.DMA((count,)),
        ],
        compiler_params=params(MOST_VMEM),
        cost_estimate=cost(0, 4 * sources[0].size * len(sources)),
        name="place",
    )(rows, *sources)


def per_device(
    tokens,
    norm_gain,
    w_qkv,
    w_mem_gates,
    persist_keys,
    persist_values,
    alpha_bias,
    eta_bias,
    w_out,
    ffn_gain,
    w_gate,
    w_up,
    w_down,
    segment_ids,
    block_table,
):
    model_dim = tokens.shape[1]
    heads, d = w_qkv.shape[1], w_mem_gates.shape[2]
    shards = lax.axis_size("head")
    n_seq = lax.axis_size("seq")
    seq_index, head_index = lax.axis_index("seq"), lax.axis_index("head")
    blocks_here = shards * tokens.shape[0] // SPAN
    per_owner = PER_OWNER

    count = tokens.shape[0] // SPAN
    cut = tokens.shape[0] // CUTS
    parts = [tokens[i * cut : (i + 1) * cut] for i in range(CUTS)] if CUTS > 1 else [tokens]
    far = [[exchange(part, "head", 2 * g) for part in parts] for g in range(1, shards // 2)]
    xs = {0: [parts, [exchange(tokens, "head", 1)]]}
    w_core = exchange(w_out, "head", 1)

    int32 = jnp.int32
    half = blocks_here // 2
    parity, place_in_line = seq_index & 1, seq_index >> 1
    id_blocks = segment_ids.reshape(-1, SPAN)[:, 0]
    keep_all = jnp.concatenate([jnp.zeros((1,), F32), (id_blocks[1:] == id_blocks[:-1]).astype(F32)])
    keep = lax.dynamic_slice_in_dim(keep_all, seq_index * blocks_here, blocks_here)
    flat = jnp.concatenate([keep, alpha_bias, eta_bias])
    seq = seq_index.astype(int32)[None]

    meta = jnp.stack([head_index, seq_index]).astype(int32)
    slots = jnp.arange(blocks_here, dtype=int32)
    line = n_seq // 2
    early = list(range(line // 2, line))
    others = list(range(1, line // 2))

    gates = jnp.broadcast_to(
        jnp.transpose(w_mem_gates, (0, 2, 1))[:, :, :, None], (heads, d, 3, d)
    ).reshape(heads, d, 3 * d)
    w = w_qkv.reshape(model_dim, heads * 3 * d)
    gain = norm_gain.reshape(1, -1)
    pkeys = persist_keys.reshape(PERS, heads, d)
    pvalues = persist_values.reshape(PERS, heads, d)
    initial = jnp.einsum("phd,phe->hde", pkeys, pvalues, preferred_element_type=F32) / PERS

    pairs = []
    groups = shards // 2
    for g in range(groups):
        if g > 0:
            far[g - 1], pairs[0]["map"], w_core = lax.optimization_barrier((far[g - 1], pairs[0]["map"], w_core))
            xs[g] = [far[g - 1], [exchange(part, "head", 1) for part in far[g - 1]]]
        pairs.append(pair_call(meta, flat, block_table if g == 0 else pairs[0]["total"], xs[g], gain, w, gates, initial, 2 * g, pairs, g == groups - 1, (half,) + (per_owner,) * (line // 2) + (half // 2,)))
    total, block_table, w_out = lax.optimization_barrier((pairs[-1]["total"], block_table, w_out))
    w_outs_far = [exchange(w_out, "head", 2 * g) for g in range(1, groups)]
    got = exchange(total, "seq", 1)

    to_me = (block_table // blocks_here == seq_index).reshape(n_seq, blocks_here)
    earlier = to_me[:, None, :] & (slots[None, None, :] < slots[None, :, None])
    sources = jnp.arange(n_seq, dtype=int32)[:, None]
    arrival = (
        jnp.sum(earlier.astype(int32), axis=2)
        + ((sources & 1) ^ parity ^ 1) * half
        + ((sources >> 1) ^ place_in_line) * per_owner
    )
    landed = (arrival.reshape(1, -1) == slots[:, None]) & to_me.reshape(1, -1)
    rows = jnp.sum(jnp.where(landed, (block_table % blocks_here)[None, :], 0), axis=1).astype(int32)

    cross, home, *same, far_same = pairs[-1]["kv"]
    far_same = exchange(far_same, "seq", line)
    a, b = join(meta, total, got)
    b, cross = lax.optimization_barrier((b, cross))
    cross = exchange(cross, "seq", 1)
    onward = [(i, i + 2) for i in range(n_seq - 2)]
    hops = n_seq // 4
    state = b
    for hop in range(hops):
        state = lax.ppermute(state, "seq", onward)
        if hop == 0:
            state, far_same, w_outs_far = lax.optimization_barrier((state, far_same, w_outs_far))
        if hop < hops - 1:
            state = step(a, b, state)
    w_outs = [w_out, w_core] + [w for one in w_outs_far for w in (one, exchange(one, "head", 1))]
    cut = lambda m: (0, m * per_owner, per_owner)
    regrouped = regroup(
        [cross, far_same] + same,
        [[(1 + m, 0, per_owner), cut(m), (1, m * per_owner, per_owner)] for m in others] + [[cut(m)] for m in early] + [[cut(0)]],
    )
    regrouped = list(regrouped)
    retrieved = list(recall(meta, got, state, pairs))
    pieces = [retrieved[0]] + [exchange(retrieved[i], "head", i) for i in range(1, shards)]
    pieces[1], regrouped = lax.optimization_barrier((pieces[1], regrouped))
    arrived = [exchange(one, "seq", 2 * m) for one, m in zip(regrouped, others + early)]
    mixed = ffn(tokens, ffn_gain.reshape(1, -1), w_outs, pieces, w_gate, w_up, w_down)
    held = [regrouped[-1], home, far_same] + arrived
    mixed, held = lax.optimization_barrier((mixed, held))
    of = lambda e, m: [e * half + m * per_owner + i for i in range(per_owner)]
    taken = [of(0, 0), of(1, 0), of(1, line // 2)]
    taken += [of(1, m) + of(0, m) + of(1, m + line // 2) for m in others] + [of(0, m) for m in early]
    return mixed, place(rows, held, taken)


def solution(mesh):
    return jax.shard_map(
        per_device,
        mesh=mesh,
        in_specs=(
            P(("seq", "head"), None),
            P(),
            P(None, "head", None),
            P("head", None, None),
            P(None, "head"),
            P(None, "head"),
            P("head"),
            P("head"),
            P("head", None),
            P(),
            P(),
            P(),
            P(),
            P(),
            P(),
        ),
        out_specs=(P(("seq", "head"), None), P("seq", None, "head")),
        check_vma=False,
    )
```
